256 devices in a mesh: seq: 64 (over z, y_hi, x), tp: 4 (over y_lo, core).
Axes of the slice: x: 4, y: 4 (y_hi: 2, y_lo: 2; y = y_hi * 2 + y_lo), z: 8, core: 2. Of those that a mesh axis runs over, the one named last changes fastest.
Arguments:
- query_rows: bfloat16 [32768, 1536], P('seq', 'tp'), may hold values from -48 to 48
- key_rows: bfloat16 [32768, 1536], P('seq', 'tp'), may hold values from -8 to 8
- value_rows: bfloat16 [32768, 1536], P('seq', 'tp'), may hold values from -6 to 6
- frame_counts: int32 [12], replicated, may hold values from 1 to 16, 128 in all
- out_weight: bfloat16 [1536, 3072], P('tp'), may hold values from -0.15625 to 0.15625
Outputs:
- mixed: bfloat16 [32768, 3072], P('seq', 'tp')
The draws below stay inside these ranges and needn't reach their ends.
Inputs may be any that keep to these rules, and one draw needn't show every extreme that they name: `frame_counts`: the 12 clips' frame counts sum to 128; the longest has exactly 16 frames.
All inputs are finite; a program needn't handle non-finite values.
Results may differ from the reference program's by a relative error of at most 0.015.
Values may be sent and summed in bfloat16 or wider, within the bound.
No kernel may reach another device: no remote copies, remote signals or barrier semaphores. Data moves between devices by JAX's collectives and lax.ppermute only.
A program may use at most 64 MiB of HBM per device.

```python
import math
import jax
import jax.numpy as jnp
import numpy as np
from jax import lax

D = 3072
HEADS = 12
RT = 16
RH = 56
RW = 56
PH = 16
PW = 16
CLIPS = 12
TOK_DEV = 512
HEAD_DIM = 128
TOKENS = 32768
FRAME = 256
FRAMES = 128
CLIP_MOST = 16


def sign_table(key):
    flips = jax.random.bernoulli(jax.random.fold_in(key, 11), 0.5, (TOKENS, HEADS * HEAD_DIM))
    return jnp.where(flips, 1.0, -1.0).astype(jnp.float32)


def draw_key_rows(key, part):
    sign_rows = sign_table(key)
    key = jax.random.fold_in(key, 1)
    extent = (TOKENS, HEADS * HEAD_DIM)
    fresh = jnp.clip(1.6 * jax.random.normal(key, extent, jnp.float32), -8.0, 8.0)
    row_phase = (jnp.arange(TOKENS, dtype=jnp.int32) % 64)[:, None]
    lead_column = (jnp.arange(HEADS * HEAD_DIM, dtype=jnp.int32) % HEAD_DIM == 0)[None, :]
    earlier_signs = jnp.roll(sign_rows, 1, axis=0)
    twin_row = jnp.where(lead_column, 0.0, 1.6 * earlier_signs)
    drawn = jnp.where(row_phase == 5, 1.6 * sign_rows, jnp.where(row_phase == 6, twin_row, fresh))
    return drawn.astype(jnp.bfloat16)


def draw_query_rows(key, part):
    key = jax.random.fold_in(key, 2)
    extent = (TOKENS, HEADS * HEAD_DIM)
    drawn = jnp.clip(1.6 * jax.random.normal(key, extent, jnp.float32), -8.0, 8.0)
    return drawn.astype(jnp.bfloat16)


def levels(key, shape, cuts, low, top_value):
    gain, own = 1.0, jax.random.fold_in(key, 6)
    for dim, parts in cuts:
        steps = jnp.exp(jax.random.uniform(jax.random.fold_in(own, dim), (parts,), jnp.float32, low / len(cuts), top_value / len(cuts)))
        gain = gain * jnp.repeat(steps, shape[dim] // parts).reshape([-1 if axis == dim else 1 for axis in range(len(shape))])
    return gain


def profile(amount, total, limit, skew):
    weights = [(1 << 20) // math.isqrt(rank ** skew) + 1 for rank in range(2, amount + 1)]
    rest, holding = total - limit - (amount - 1), [1] * (amount - 1)
    while rest > 0:
        movable = [i for i in range(amount - 1) if holding[i] < limit]
        whole, left = sum([weights[i] for i in movable]), rest
        for i in movable:
            extra = min(limit - holding[i], max(1, left * weights[i] // whole), rest)
            holding[i] = holding[i] + extra
            rest = rest - extra
    return np.array([limit] + holding)


def uneven(key, number_of, total, reach, skew):
    if number_of == 2:
        one = jax.random.randint(key, (), max(1, total - reach), min(reach, total - 1) + 1)
        return jnp.stack([one, total - one])
    tallies = jnp.asarray(profile(number_of, total, reach, skew), jnp.int32)
    couples = (number_of - 1) // 2
    giver, taker = tallies[1:1 + 2 * couples:2], tallies[2:2 + 2 * couples:2]
    room = jnp.minimum(giver - 1, reach - taker)
    moved = jax.random.randint(jax.random.fold_in(key, 1), (couples,), 0, 1 << 20) % (room + 1)
    tallies = tallies.at[1:1 + 2 * couples:2].set(giver - moved).at[2:2 + 2 * couples:2].set(taker + moved)
    return tallies[jax.random.permutation(jax.random.fold_in(key, 2), number_of)]


def centred(own_key, dims, spread, reach, split=(), kind=jnp.bfloat16):
    gain = levels(own_key, dims, split, -0.22, 0.18) if split else 1.0
    values = jax.random.normal(own_key, dims, jnp.float32) * spread * gain
    return jnp.minimum(jnp.maximum(values, -reach), reach).astype(kind)


def setup_inputs(seed: int = 0) -> dict:
    keys = jax.random.split(jax.random.key(seed), 6)
    query_rows = draw_query_rows(jax.random.fold_in(keys[5], 71), 0)
    key_rows = draw_key_rows(jax.random.fold_in(keys[5], 71), 0)
    value_rows = centred(keys[2], (TOKENS, HEADS * HEAD_DIM), 1.0, 6.0, ((0, 64), (1, 4)))
    frame_counts = uneven(keys[3], CLIPS, FRAMES, CLIP_MOST, 2).astype(jnp.int32)
    out_weight = centred(keys[4], (HEADS * HEAD_DIM, D), (HEADS * HEAD_DIM) ** -0.5, 0.15625, ((0, 4),))
    return {"query_rows": query_rows, "key_rows": key_rows, "value_rows": value_rows, "frame_counts": frame_counts, "out_weight": out_weight}


NEG_FILL = -1e30
ROPE_BASE = 256.0


def clip_layout(frame_counts, token_index):
    clip_sizes = frame_counts * (PH * PW)
    clip_ends = jnp.cumsum(clip_sizes)
    passed = token_index[:, None] >= clip_ends[None, :]
    clip_id = jnp.sum(passed.astype(jnp.int32), axis=1)
    clip_start = jnp.sum(jnp.where(passed, clip_sizes[None, :], 0), axis=1)
    return clip_id, token_index - clip_start


def rotate(features, offset):
    frame_size = PH * PW
    coordinates = (offset // frame_size, (offset % frame_size) // PW, offset % PW)
    pieces = []
    section_start = 0
    for section_width, coordinate in zip((RT, RH, RW), coordinates):
        half_width = section_width // 2
        section = features[:, :, section_start:section_start + section_width]
        first_half = section[..., :half_width]
        second_half = section[..., half_width:]
        frequency = jnp.exp(-(2.0 * jnp.arange(half_width, dtype=jnp.float32) / section_width) * math.log(ROPE_BASE))
        phase_angle = coordinate.astype(jnp.float32)[:, None] * frequency[None, :]
        cosine = jnp.cos(phase_angle)[:, None, :]
        sine_part = jnp.sin(phase_angle)[:, None, :]
        pieces.append(first_half * cosine - second_half * sine_part)
        pieces.append(second_half * cosine + first_half * sine_part)
        section_start = section_start + section_width
    return jnp.concatenate(pieces, axis=2)


def reference(query_rows, key_rows, value_rows, frame_counts, out_weight):
    token_index = jnp.arange(TOKENS, dtype=jnp.int32)
    clip_id, offset = clip_layout(frame_counts, token_index)
    rotated_q = rotate(query_rows.astype(jnp.float32).reshape(TOKENS, HEADS, HEAD_DIM), offset).astype(jnp.bfloat16)
    rotated_k = rotate(key_rows.astype(jnp.float32).reshape(TOKENS, HEADS, HEAD_DIM), offset).astype(jnp.bfloat16)
    rotated_q = lax.optimization_barrier(rotated_q)
    rotated_k = lax.optimization_barrier(rotated_k)
    value_heads = value_rows.reshape(TOKENS, HEADS, HEAD_DIM)
    reach_tokens = CLIP_MOST * FRAME
    key_padded = jnp.pad(rotated_k, ((reach_tokens, reach_tokens), (0, 0), (0, 0)))
    value_padded = jnp.pad(value_heads, ((reach_tokens, reach_tokens), (0, 0), (0, 0)))
    clip_padded = jnp.pad(clip_id, (reach_tokens, reach_tokens), constant_values=-1)
    span_tokens = TOK_DEV + 2 * reach_tokens
    scale_factor = HEAD_DIM ** -0.5

    def block(block_index):
        lower = (block_index * TOK_DEV).astype(jnp.int32)
        query_block = lax.dynamic_slice_in_dim(rotated_q, lower, TOK_DEV, 0).astype(jnp.float32)
        key_block = lax.dynamic_slice_in_dim(key_padded, lower, span_tokens, 0).astype(jnp.float32)
        value_block = lax.dynamic_slice_in_dim(value_padded, lower, span_tokens, 0).astype(jnp.float32)
        query_clip = lax.dynamic_slice_in_dim(clip_id, lower, TOK_DEV, 0)
        key_clip = lax.dynamic_slice_in_dim(clip_padded, lower, span_tokens, 0)
        scores = jnp.einsum("qhd,khd->hqk", query_block, key_block) * scale_factor
        allowed = query_clip[:, None] == key_clip[None, :]
        scores = jnp.where(allowed[None], scores, NEG_FILL)
        row_max = jnp.max(scores, axis=2, keepdims=True)
        expo = jnp.where(allowed[None], jnp.exp(scores - row_max), 0.0)
        total = jnp.sum(expo, axis=2)
        weights = lax.optimization_barrier(expo.astype(jnp.bfloat16)).astype(jnp.float32)
        summed = jnp.einsum("hqk,khd->hqd", weights, value_block) / total[:, :, None]
        return summed.transpose(1, 0, 2).reshape(TOK_DEV, HEADS * HEAD_DIM).astype(jnp.bfloat16)

    attended = lax.map(block, jnp.arange(TOKENS // TOK_DEV, dtype=jnp.int32)).reshape(TOKENS, HEADS * HEAD_DIM)
    return jnp.dot(attended, out_weight, preferred_element_type=jnp.float32).astype(jnp.bfloat16)
```

```python
import math

import jax
import jax.numpy as jnp
import numpy as np
from jax import lax
from jax.experimental import pallas as pl
from jax.experimental.pallas import tpu as pltpu
from jax.sharding import Mesh
from jax.sharding import PartitionSpec as P

RT = 16
RH = 56
RW = 56
PH = 16
PW = 16
FRAME = PH * PW
HEAD_DIM = 128
CLIPS = 12
TOK = 512
SLOTS = 16
ROPE_BASE = 256.0
NEG = -1e30
EXP_SCALE = HEAD_DIM ** (-0.5) * math.log2(math.e)

GROUPS = ((0, 1, 2),)
STEPS = (0, -1, 1, 2)


def rope_tables():
    freq = np.zeros(HEAD_DIM)
    swap = np.zeros((HEAD_DIM, HEAD_DIM), np.float32)
    sign = np.zeros(HEAD_DIM)
    base = 0
    bounds = []
    for width in (RT, RH, RW):
        half = width // 2
        f = np.exp(-(2.0 * np.arange(half) / width) * math.log(ROPE_BASE))
        freq[base : base + half] = f
        freq[base + half : base + width] = f
        sign[base : base + half] = -1.0
        sign[base + half : base + width] = 1.0
        for j in range(half):
            swap[base + half + j, base + j] = 1.0
            swap[base + j, base + half + j] = 1.0
        bounds.append((base, base + width))
        base += width
    token = np.arange(FRAME)
    angle = np.zeros((FRAME, HEAD_DIM))
    (t0, t1), (h0, h1), (w0, w1) = bounds
    angle[:, h0:h1] = (token // PW)[:, None] * freq[None, h0:h1]
    angle[:, w0:w1] = (token % PW)[:, None] * freq[None, w0:w1]
    angle_t = np.zeros((SLOTS, HEAD_DIM))
    angle_t[:, t0:t1] = np.arange(SLOTS)[:, None] * freq[None, t0:t1]
    space = np.stack([np.cos(angle), np.sin(angle) * sign]).astype(np.float32)
    time = np.stack([np.cos(angle_t), np.sin(angle_t) * sign]).astype(np.float32)
    return space, time, swap


def clip_bounds(meta_ref, frame):
    start = jnp.int32(0)
    end = jnp.int32(0)
    total = jnp.int32(0)
    for c in range(CLIPS):
        here = frame >= total
        total = total + meta_ref[c]
        start = jnp.where(here, total - meta_ref[c], start)
        end = jnp.where(here, total, end)
    return start, end


def dot_nt(a, b):
    return lax.dot_general(a, b, (((1,), (1,)), ((), ())), preferred_element_type=jnp.float32)


def dot_nn(a, b):
    return lax.dot_general(a, b, (((1,), (0,)), ((), ())), preferred_element_type=jnp.float32)


def prepare_kernel(meta_ref, q_ref, k_ref, v_ref, space_ref, time_ref, swap_ref, *outs):
    swap = swap_ref[0]
    eye = swap_ref[1]
    first = meta_ref[CLIPS] * SLOTS + meta_ref[CLIPS + 1] * 8 + meta_ref[CLIPS + 2] * 2
    lane = lax.broadcasted_iota(jnp.int32, (FRAME, HEAD_DIM), 1)
    for e in range(2):
        start, _ = clip_bounds(meta_ref, first + e)
        t = first + e - start
        tok = slice(FRAME * e, FRAME * (e + 1))
        cos = jnp.where(lane < RT, time_ref[0, pl.ds(t, 1), :], space_ref[0])
        sin = jnp.where(lane < RT, time_ref[1, pl.ds(t, 1), :], space_ref[1])
        cos_t = cos.T
        sin_t = sin.T
        for g, heads in enumerate(GROUPS):
            q_out, kv_out = outs[2 * g], outs[2 * g + 1]
            n = len(heads)
            for a, h in enumerate(heads):
                col = slice(HEAD_DIM * h, HEAD_DIM * (h + 1))
                row = slice(HEAD_DIM * a, HEAD_DIM * (a + 1))
                vrow = slice(HEAD_DIM * (n + a), HEAD_DIM * (n + a + 1))
                k = k_ref[tok, col]
                rot = (k.astype(jnp.float32) * cos + dot_nn(k, swap) * sin).astype(jnp.bfloat16)
                kv_out[row, FRAME * e : FRAME * e + 128] = rot[:128]
                kv_out[row, FRAME * e + 128 : FRAME * e + 256] = rot[128:]
                kv_out[vrow, tok] = dot_nt(eye, v_ref[tok, col]).astype(jnp.bfloat16)
                q = q_ref[tok, col]
                rot = dot_nt(eye, q) * cos_t + dot_nt(swap, q) * sin_t
                q_out[row, tok] = rot.astype(jnp.bfloat16)


def split3(value):
    hi = value.astype(jnp.bfloat16)
    rest = value - hi.astype(jnp.float32)
    mid = rest.astype(jnp.bfloat16)
    low = (rest - mid.astype(jnp.float32)).astype(jnp.bfloat16)
    return [hi, mid, low]


def attend_kernel(n, meta_ref, q0, q1, q2, q3, own, ypair, zm, zp, third, o0, o1, o2, o3, kv, sem):
    blocks = (zm, own, zp, third, ypair)
    copies = [pltpu.make_async_copy(b, kv.at[i], sem.at[i]) for i, b in enumerate(blocks)]
    for c in copies:
        c.start()
    z, yh, x = meta_ref[CLIPS], meta_ref[CLIPS + 1], meta_ref[CLIPS + 2]
    plane = z * SLOTS
    for c in copies:
        c.wait()
    for r, (q_ref, o_ref) in enumerate(zip((q0, q1, q2, q3), (o0, o1, o2, o3))):
        xq = lax.rem(x + STEPS[r] + 4, 4)
        stats = [[None, None] for _ in range(n)]
        for e in range(2):
            frame = plane + yh * 8 + xq * 2 + e
            start, end = clip_bounds(meta_ref, frame)
            places = []
            for sl in range(4):
                row = yh if sl < 2 else 1 - yh
                mid = plane + row * 8 + x * 2 + sl % 2
                before = mid - SLOTS >= start
                inside = (mid >= start) & (mid < end)
                after = mid + SLOTS < end
                if sl < 2:
                    src = jnp.where(inside, 1, jnp.where(before, 0, 2))
                else:
                    src = jnp.where(inside, 4, 3)
                valid = before | inside | after
                places.append((src, valid))
            some = places[0][1] | places[1][1] | places[2][1] | places[3][1]
            tok = slice(FRAME * e, FRAME * (e + 1))
            for a in range(n):
                row = slice(HEAD_DIM * a, HEAD_DIM * (a + 1))
                vrow = slice(HEAD_DIM * (n + a), HEAD_DIM * (n + a + 1))
                qt = q_ref[row, tok]
                scores = []
                top = None
                for sl in range(4):
                    src, valid = places[sl]
                    bias = jnp.where(valid, 0.0, NEG)
                    for half in range(2):
                        lo = FRAME * (sl % 2) + 128 * half
                        s = dot_nn(kv[src, row, lo : lo + 128], qt)
                        scores.append((s, bias))
                        peak = jnp.max(s, axis=0, keepdims=True) * EXP_SCALE + bias
                        top = peak if top is None else jnp.maximum(top, peak)
                acc = None
                total = None
                for sl in range(4):
                    src, _ = places[sl]
                    parts = []
                    for half in range(2):
                        s, bias = scores[2 * sl + half]
                        shift = jnp.where(some, bias - top, NEG)
                        p = jnp.exp2(s * EXP_SCALE + shift)
                        add = jnp.sum(p, axis=0, keepdims=True)
                        total = add if total is None else total + add
                        parts.append(p.astype(jnp.bfloat16))
                    weights = jnp.concatenate(parts, axis=0)
                    lo = FRAME * (sl % 2)
                    term = dot_nn(kv[src, vrow, lo : lo + FRAME], weights)
                    acc = term if acc is None else acc + term
                total = jnp.maximum(total, 1e-30)
                o_ref[row, tok] = (acc * (1.0 / total)).astype(jnp.bfloat16)
                stats[a][e] = jnp.where(some, top + jnp.log2(total), NEG)
        rows = []
        for a in range(n):
            rows += split3(jnp.concatenate(stats[a], axis=1))
        rows.append(jnp.zeros((16 - len(rows), TOK), jnp.bfloat16))
        o_ref[HEAD_DIM * n : HEAD_DIM * n + 16, :] = jnp.concatenate(rows, axis=0)


def merge_kernel(n, p0, p1, p2, p3, out):
    parts = (p0, p1, p2, p3)
    for a in range(n):
        row = slice(HEAD_DIM * a, HEAD_DIM * (a + 1))
        levels = []
        for p in parts:
            tail = p[HEAD_DIM * n : HEAD_DIM * n + 16, :].astype(jnp.float32)
            levels.append(tail[3 * a : 3 * a + 1] + tail[3 * a + 1 : 3 * a + 2] + tail[3 * a + 2 : 3 * a + 3])
        top = jnp.maximum(jnp.maximum(levels[0], levels[1]), jnp.maximum(levels[2], levels[3]))
        shares = [jnp.exp2(v - top) for v in levels]
        inv = 1.0 / (shares[0] + shares[1] + shares[2] + shares[3])
        acc = None
        for p, s in zip(parts, shares):
            term = p[row, :].astype(jnp.float32) * (s * inv)
            acc = term if acc is None else acc + term
        out[:, row] = acc.T.astype(jnp.bfloat16)


def project_kernel(count, *refs):
    sides, weights, out = refs[:count], refs[count : 2 * count], refs[2 * count]
    acc = None
    for s, w in zip(sides, weights):
        term = dot_nn(s[...], w[...])
        acc = term if acc is None else acc + term
    out[...] = acc.astype(jnp.bfloat16)


VMEM = pl.BlockSpec(memory_space=pltpu.VMEM)
SMEM = pl.BlockSpec(memory_space=pltpu.SMEM)
ANY = pl.BlockSpec(memory_space=pl.ANY)
PARAMS = pltpu.CompilerParams(vmem_limit_bytes=48 * 1024 * 1024)


def cost(flops, size, trans=0):
    return pl.CostEstimate(flops=flops, bytes_accessed=size, transcendentals=trans)


def shift(value, axis, by):
    count = lax.axis_size(axis)
    return lax.ppermute(value, axis, [(i, (i + by) % count) for i in range(count)])


def flip(value, axis):
    return lax.ppermute(value, axis, [(0, 1), (1, 0)])


def per_device(query_rows, key_rows, value_rows, frame_counts, out_weight):
    place = jnp.stack([lax.axis_index("z"), lax.axis_index("yh"), lax.axis_index("x"), 0])
    meta = jnp.concatenate([frame_counts, place.astype(jnp.int32)])
    space, time, swap = rope_tables()
    mats = jnp.asarray(np.stack([swap, np.eye(HEAD_DIM, dtype=np.float32)]), jnp.bfloat16)

    shapes = []
    for heads in GROUPS:
        n = len(heads)
        shapes.append(jax.ShapeDtypeStruct((n * HEAD_DIM, TOK), jnp.bfloat16))
        shapes.append(jax.ShapeDtypeStruct((2 * n * HEAD_DIM, TOK), jnp.bfloat16))
    prepared = pl.pallas_call(
        prepare_kernel,
        out_shape=shapes,
        in_specs=[SMEM] + [VMEM] * 6,
        out_specs=[VMEM] * len(shapes),
        compiler_params=PARAMS,
        cost_estimate=cost(200_000_000, 3_000_000),
        name="prepare",
    )(meta, query_rows, key_rows, value_rows, jnp.asarray(space), jnp.asarray(time), mats)

    arrived = []
    zy = [((zi * 2), ((zi + 1) % 8) * 2) for zi in range(8)]
    zy += [((zi * 2 + 1), ((zi - 1) % 8) * 2 + 1) for zi in range(8)]
    for g, heads in enumerate(GROUPS):
        q, kv = prepared[2 * g], prepared[2 * g + 1]
        ypair = flip(kv, "yh")
        zm = shift(kv, "z", 1)
        zp = shift(kv, "z", -1)
        qs = [q, shift(q, "x", 1), shift(q, "x", -1), shift(q, "x", 2)]
        third = lax.ppermute(ypair, ("z", "yh"), zy)
        arrived.append((qs, [kv, ypair, zm, zp, third]))

    tp = lax.axis_index("yl") * 2 + lax.axis_index("core")
    cols = out_weight.shape[1] // 4

    def mine(j):
        return lax.dynamic_slice_in_dim(out_weight, j * cols, cols, 1)

    w_own = mine(tp)
    w_core = flip(mine(tp ^ 1), "core")
    w_yl = flip(mine(tp ^ 2), "yl")
    w_far = lax.ppermute(mine(tp ^ 3), ("yh", "yl", "core"), [(i, 7 - i) for i in range(8)])

    sides = []
    for g, heads in enumerate(GROUPS):
        n = len(heads)
        qs, kvs = arrived[g]
        out = jax.ShapeDtypeStruct((n * HEAD_DIM + 16, TOK), jnp.bfloat16)
        partial = pl.pallas_call(
            lambda *refs, n=n: attend_kernel(n, *refs),
            out_shape=[out] * 4,
            in_specs=[SMEM] + [VMEM] * 4 + [ANY] * 5,
            out_specs=[VMEM] * 4,
            scratch_shapes=[
                pltpu.VMEM((5, 2 * n * HEAD_DIM, TOK), jnp.bfloat16),
                pltpu.SemaphoreType.DMA((5,)),
            ],
            compiler_params=PARAMS,
            cost_estimate=cost(n * 3_200_000_000, n * 2_000_000, n * 2_000_000),
            name="attend",
        )(meta, *qs, *kvs)
        back = [partial[0]] + [shift(partial[r], "x", STEPS[r]) for r in (1, 2, 3)]
        att = pl.pallas_call(
            lambda *refs, n=n: merge_kernel(n, *refs),
            out_shape=jax.ShapeDtypeStruct((TOK, n * HEAD_DIM), jnp.bfloat16),
            in_specs=[VMEM] * 4,
            out_specs=VMEM,
            compiler_params=PARAMS,
            cost_estimate=cost(n * 10_000_000, n * 700_000),
            name="merge",
        )(*back)
        att_yl = flip(att, "yl")
        att_core = flip(att, "core")
        att_far = flip(att_yl, "core")
        sides.append((att, att_core, att_yl, att_far))

    terms, weights = [], []
    for g, heads in enumerate(GROUPS):
        rows = slice(heads[0] * HEAD_DIM, (heads[-1] + 1) * HEAD_DIM)
        for s, w in zip(sides[g], (w_own, w_core, w_yl, w_far)):
            terms.append(s)
            weights.append(w if len(GROUPS) == 1 else w[rows])
    tile = 256
    return pl.pallas_call(
        lambda *refs: project_kernel(len(terms), *refs),
        grid=(TOK // tile,),
        out_shape=jax.ShapeDtypeStruct((TOK, cols), jnp.bfloat16),
        in_specs=[pl.BlockSpec((tile, s.shape[1]), lambda i: (i, 0)) for s in terms]
        + [pl.BlockSpec(w.shape, lambda i: (0, 0)) for w in weights],
        out_specs=pl.BlockSpec((tile, cols), lambda i: (i, 0)),
        compiler_params=PARAMS,
        cost_estimate=cost(1_200_000_000, 4_700_000),
        name="project",
    )(*terms, *weights)


def solution(mesh):
    fine = Mesh(mesh.devices.reshape(8, 2, 4, 2, 2), ("z", "yh", "x", "yl", "core"))
    seq, tp = ("z", "yh", "x"), ("yl", "core")
    return jax.shard_map(
        per_device,
        mesh=fine,
        in_specs=(P(seq, tp), P(seq, tp), P(seq, tp), P(), P(tp, None)),
        out_specs=P(seq, tp),
        check_vma=False,
    )
```

```python
import math

import jax
import jax.numpy as jnp
import numpy as np
from jax import lax
from jax.experimental import pallas as pl
from jax.experimental.pallas import tpu as pltpu
from jax.sharding import Mesh
from jax.sharding import PartitionSpec as P

RT = 16
RH = 56
RW = 56
PH = 16
PW = 16
FRAME = PH * PW
HEAD_DIM = 128
CLIPS = 12
HEADS = 3
TOK = 512
SLOTS = 16
ROPE_BASE = 256.0
NEG = -1e30
EXP_SCALE = HEAD_DIM ** (-0.5) * math.log2(math.e)

STEPS = (0, -1, 1, 2)
CALLS = ((3, 0), (1, 2))


def rope_tables():
    freq = np.zeros(HEAD_DIM)
    swap = np.zeros((HEAD_DIM, HEAD_DIM), np.float32)
    sign = np.zeros(HEAD_DIM)
    base = 0
    bounds = []
    for width in (RT, RH, RW):
        half = width // 2
        f = np.exp(-(2.0 * np.arange(half) / width) * math.log(ROPE_BASE))
        freq[base : base + half] = f
        freq[base + half : base + width] = f
        sign[base : base + half] = -1.0
        sign[base + half : base + width] = 1.0
        for j in range(half):
            swap[base + half + j, base + j] = 1.0
            swap[base + j, base + half + j] = 1.0
        bounds.append((base, base + width))
        base += width
    token = np.arange(FRAME)
    angle = np.zeros((FRAME, HEAD_DIM))
    (t0, t1), (h0, h1), (w0, w1) = bounds
    angle[:, h0:h1] = (token // PW)[:, None] * freq[None, h0:h1]
    angle[:, w0:w1] = (token % PW)[:, None] * freq[None, w0:w1]
    angle_t = np.zeros((SLOTS, HEAD_DIM))
    angle_t[:, t0:t1] = np.arange(SLOTS)[:, None] * freq[None, t0:t1]
    space = np.stack([np.cos(angle), np.sin(angle) * sign]).astype(np.float32)
    time = np.stack([np.cos(angle_t), np.sin(angle_t) * sign]).astype(np.float32)
    return space, time, swap


def here():
    return lax.axis_index("z"), lax.axis_index("yh"), lax.axis_index("x")


def clip_bounds(counts_ref, frame):
    start = jnp.int32(0)
    end = jnp.int32(0)
    total = jnp.int32(0)
    for c in range(CLIPS):
        past = frame >= total
        before = total
        total = total + counts_ref[c]
        start = jnp.where(past, before, start)
        end = jnp.where(past, total, end)
    return start, end


def dot_nt(a, b):
    return lax.dot_general(a, b, (((1,), (1,)), ((), ())), preferred_element_type=jnp.float32)


def dot_nn(a, b):
    return lax.dot_general(a, b, (((1,), (0,)), ((), ())), preferred_element_type=jnp.float32)


def prepare_kernel(counts_ref, q_hbm, k_hbm, v_hbm, space_hbm, time_hbm, swap_hbm, q_out, kv_out, *refs):
    bufs, (kv_buf, q_buf, sem) = refs[:-3], refs[-3:]
    sources = (k_hbm, space_hbm, time_hbm, swap_hbm, v_hbm, q_hbm)
    copies = [pltpu.make_async_copy(s, d, sem.at[i]) for i, (s, d) in enumerate(zip(sources, bufs))]
    for c in copies:
        c.start()
    k_ref, space_ref, time_ref, swap_ref, v_ref, q_ref = bufs
    z, yh, x = here()
    first = z * SLOTS + yh * 8 + x * 2
    times = []
    for e in range(2):
        start, _ = clip_bounds(counts_ref, first + e)
        times.append(jnp.clip(first + e - start, 0, SLOTS - 1))
    for c in copies[:4]:
        c.wait()
    swap = swap_ref[0]
    eye = swap_ref[1]
    lane = lax.broadcasted_iota(jnp.int32, (FRAME, HEAD_DIM), 1)
    tables = []
    for e in range(2):
        cos = jnp.where(lane < RT, time_ref[0, pl.ds(times[e], 1), :], space_ref[0])
        sin = jnp.where(lane < RT, time_ref[1, pl.ds(times[e], 1), :], space_ref[1])
        tables.append((cos, sin))
    parts = [
        (e, h, slice(FRAME * e, FRAME * (e + 1)), slice(HEAD_DIM * h, HEAD_DIM * (h + 1)))
        for h in range(HEADS)
        for e in range(2)
    ]
    for e, h, tok, col in parts:
        cos, sin = tables[e]
        k = k_ref[tok, col]
        rot = ((k.astype(jnp.float32) * cos + dot_nn(k, swap) * sin) * EXP_SCALE).astype(jnp.bfloat16)
        kv_buf[col, FRAME * e : FRAME * e + 128] = rot[:128]
        kv_buf[col, FRAME * e + 128 : FRAME * e + 256] = rot[128:]
    outs = [pltpu.make_async_copy(kv_buf.at[pl.ds(0, HEADS * HEAD_DIM)], kv_out.at[pl.ds(0, HEADS * HEAD_DIM)], sem.at[6])]
    outs[0].start()
    copies[4].wait()
    for e, h, tok, col in parts:
        kv_buf[HEAD_DIM * (HEADS + h) : HEAD_DIM * (HEADS + h + 1), tok] = dot_nt(eye, v_ref[tok, col]).astype(jnp.bfloat16)
    values = pl.ds(HEADS * HEAD_DIM, HEADS * HEAD_DIM)
    outs.append(pltpu.make_async_copy(kv_buf.at[values], kv_out.at[values], sem.at[7]))
    outs[1].start()
    copies[5].wait()
    turned = [(cos.T, sin.T) for cos, sin in tables]
    for e, h, tok, col in parts:
        cos, sin = turned[e]
        q = q_ref[tok, col]
        q_buf[col, tok] = (dot_nt(eye, q) * cos + dot_nt(swap, q) * sin).astype(jnp.bfloat16)
    outs.append(pltpu.make_async_copy(q_buf, q_out, sem.at[8]))
    outs[2].start()
    for c in outs:
        c.wait()


def stage_kernel(q_hbm, kv_hbm, q_out, kv_out, sem):
    copies = [
        pltpu.make_async_copy(q_hbm, q_out, sem.at[0]),
        pltpu.make_async_copy(kv_hbm, kv_out, sem.at[1]),
    ]
    for c in copies:
        c.start()
    for c in copies:
        c.wait()


def split3(value):
    hi = value.astype(jnp.bfloat16)
    rest = value - hi.astype(jnp.float32)
    mid = rest.astype(jnp.bfloat16)
    low = (rest - mid.astype(jnp.float32)).astype(jnp.bfloat16)
    return [hi, mid, low]


def fold(value, op):
    out = value[0:8]
    for i in range(8, value.shape[0], 8):
        out = op(out, value[i : i + 8])
    return out


def attend_kernel(steps, final, counts_ref, *refs):
    n, count = HEADS, len(steps)
    q_refs, refs = refs[:count], refs[count:]
    kv_refs, refs = refs[:3], refs[3:]
    if final:
        near_ref, refs = refs[0], refs[1:]
        o_refs, (kv,) = refs[:count], refs[count:]
    else:
        near_ref, kv = refs

    def load(a):
        for part in range(2):
            row = slice(HEAD_DIM * (n * part + a), HEAD_DIM * (n * part + a + 1))
            if final:
                kv[0, row, :] = kv_refs[0][row, :]
                kv[1, row, :] = kv_refs[1 + part][HEAD_DIM * a : HEAD_DIM * (a + 1), :]
            else:
                for i in range(3):
                    kv[i, row, :] = kv_refs[i][row, :]

    z, yh, x = here()
    plane = z * SLOTS
    tables = []
    for r in range(count):
        xq = lax.rem(x + steps[r] + 4, 4)
        for e in range(2):
            start, end = clip_bounds(counts_ref, plane + yh * 8 + xq * 2 + e)
            places = []
            for sl in range(2):
                row = 1 - yh if final else yh
                mid = plane + row * 8 + x * 2 + sl
                before = mid - SLOTS >= start
                inside = (mid >= start) & (mid < end)
                after = mid + SLOTS < end
                if final:
                    src = jnp.where(inside, 0, 1)
                else:
                    src = jnp.where(inside, 1, jnp.where(before, 0, 2))
                valid = before | inside | after
                places.append((src, jnp.where(valid, 0.0, NEG), valid))
            tables.append((places, places[0][2] | places[1][2]))
    units = [(a, r, e) for a in range(n) for r in range(count) for e in range(2)]
    state, stats = {}, {}

    def scores(u, sl):
        a, r, e = units[u]
        if sl == 0 and r == 0 and e == 0:
            load(a)
        src, bias, _ = tables[2 * r + e][0][sl]
        row = slice(HEAD_DIM * a, HEAD_DIM * (a + 1))
        lo = FRAME * sl
        keys = jnp.concatenate([kv[src, row, lo : lo + 128], kv[src, row, lo + 128 : lo + 256]], axis=0)
        s = dot_nn(keys, q_refs[r][row, FRAME * e : FRAME * (e + 1)])
        peak = fold(s, jnp.maximum) + bias
        st = state.setdefault(u, {"s": {}})
        st["s"][sl] = s
        st["top"] = peak if sl == 0 else jnp.maximum(st["top"], peak)

    def weigh(u, sl):
        a, r, e = units[u]
        places, some = tables[2 * r + e]
        src, bias, _ = places[sl]
        st = state[u]
        p = jnp.exp2(st["s"].pop(sl) + jnp.where(some, bias - st["top"], NEG))
        add = fold(p, jnp.add)
        row = slice(HEAD_DIM * (n + a), HEAD_DIM * (n + a + 1))
        term = dot_nn(kv[src, row, FRAME * sl : FRAME * (sl + 1)], p.astype(jnp.bfloat16))
        st["total"] = add if sl == 0 else st["total"] + add
        st["acc"] = term if sl == 0 else st["acc"] + term

    def top(u):
        state[u]["top"] = jnp.max(state[u]["top"], axis=0, keepdims=True)

    for sl in range(2):
        scores(0, sl)
    top(0)
    for u, (a, r, e) in enumerate(units):
        for sl in range(2):
            if u + 1 < len(units):
                scores(u + 1, sl)
            weigh(u, sl)
        if u + 1 < len(units):
            top(u + 1)
        st = state.pop(u)
        total = jnp.sum(st["total"], axis=0, keepdims=True)
        peak = jnp.where(tables[2 * r + e][1], st["top"], NEG)
        row = slice(HEAD_DIM * a, HEAD_DIM * (a + 1))
        tok = slice(FRAME * e, FRAME * (e + 1))
        peak_row = slice(HEAD_DIM * n + 8 * a, HEAD_DIM * n + 8 * a + 1)
        total_row = slice(HEAD_DIM * n + 8 * a + 1, HEAD_DIM * n + 8 * a + 2)
        if final:
            block = STEPS.index(steps[r])
            near_peak = near_ref[block, peak_row, tok]
            both = jnp.maximum(peak, near_peak)
            far_part = jnp.exp2(peak - both)
            near_part = jnp.exp2(near_peak - both)
            total = total * far_part + near_ref[block, total_row, tok] * near_part
            total = jnp.maximum(total, 1e-30)
            inv = 1.0 / total
            acc = st["acc"] * (far_part * inv) + near_ref[block, row, tok] * (near_part * inv)
            o_refs[r][row, tok] = acc.astype(jnp.bfloat16)
            stats[r, a, e] = both + jnp.log2(total)
        else:
            near_ref[r, row, tok] = st["acc"]
            near_ref[r, peak_row, tok] = peak
            near_ref[r, total_row, tok] = total
    if final:
        for r in range(count):
            rows = []
            for a in range(n):
                rows += split3(jnp.concatenate([stats[r, a, 0], stats[r, a, 1]], axis=1))
            rows.append(jnp.zeros((16 - len(rows), TOK), jnp.bfloat16))
            o_refs[r][HEAD_DIM * n : HEAD_DIM * n + 16, :] = jnp.concatenate(rows, axis=0)


def level(ref, a):
    base = HEAD_DIM * HEADS
    tail = ref[base : base + 16, :].astype(jnp.float32)
    return tail[3 * a : 3 * a + 1] + tail[3 * a + 1 : 3 * a + 2] + tail[3 * a + 2 : 3 * a + 3]


def merge_two_kernel(p0, p1, out):
    for a in range(HEADS):
        row = slice(HEAD_DIM * a, HEAD_DIM * (a + 1))
        one, two = level(p0, a), level(p1, a)
        top = jnp.maximum(one, two)
        one, two = jnp.exp2(one - top), jnp.exp2(two - top)
        inv = 1.0 / (one + two)
        out[row, :] = p0[row, :].astype(jnp.float32) * (one * inv) + p1[row, :].astype(jnp.float32) * (two * inv)
        out[HEAD_DIM * HEADS + 8 * a : HEAD_DIM * HEADS + 8 * a + 1, :] = top + jnp.log2(one + two)


def merge_last_kernel(m, p0, p1, out):
    for a in range(HEADS):
        row = slice(HEAD_DIM * a, HEAD_DIM * (a + 1))
        base = HEAD_DIM * HEADS + 8 * a
        levels = [m[base : base + 1, :], level(p0, a), level(p1, a)]
        top = jnp.maximum(jnp.maximum(levels[0], levels[1]), levels[2])
        shares = [jnp.exp2(v - top) for v in levels]
        inv = 1.0 / (shares[0] + shares[1] + shares[2])
        acc = None
        for p, s in zip((m, p0, p1), shares):
            term = p[row, :].astype(jnp.float32) * (s * inv)
            acc = term if acc is None else acc + term
        out[:, row] = acc.T.astype(jnp.bfloat16)


def project_kernel(*refs):
    refs, out = refs[:-1], refs[-1]
    acc = None
    if len(refs) % 2:
        acc, refs = refs[0][...], refs[1:]
    for i in range(0, len(refs), 2):
        term = dot_nn(refs[i][...], refs[i + 1][...])
        acc = term if acc is None else acc + term
    out[...] = acc.astype(out.dtype)


VMEM = pl.BlockSpec(memory_space=pltpu.VMEM)
SMEM = pl.BlockSpec(memory_space=pltpu.SMEM)
HBM = pl.BlockSpec(memory_space=pltpu.HBM)


def params(mib):
    return pltpu.CompilerParams(vmem_limit_bytes=mib * 1024 * 1024)


def cost(flops, size, trans=0):
    return pl.CostEstimate(flops=flops, bytes_accessed=size, transcendentals=trans)


def shift(value, axis, by):
    count = lax.axis_size(axis)
    return lax.ppermute(value, axis, [(i, (i + by) % count) for i in range(count)])


def flip(value, axis):
    return lax.ppermute(value, axis, [(0, 1), (1, 0)])


def per_device(query_rows, key_rows, value_rows, frame_counts, out_weight):
    space, time, swap = rope_tables()
    mats = np.stack([swap, np.eye(HEAD_DIM)]).astype(jnp.bfloat16)
    feats = HEADS * HEAD_DIM
    q, kv = pl.pallas_call(
        prepare_kernel,
        out_shape=[jax.ShapeDtypeStruct((size, TOK), jnp.bfloat16) for size in (feats, 2 * feats)],
        in_specs=[SMEM] + [HBM] * 6,
        out_specs=[HBM] * 2,
        scratch_shapes=[
            pltpu.VMEM(key_rows.shape, jnp.bfloat16),
            pltpu.VMEM(space.shape, jnp.float32),
            pltpu.VMEM(time.shape, jnp.float32),
            pltpu.VMEM(mats.shape, jnp.bfloat16),
            pltpu.VMEM(key_rows.shape, jnp.bfloat16),
            pltpu.VMEM(key_rows.shape, jnp.bfloat16),
            pltpu.VMEM((2 * feats, TOK), jnp.bfloat16),
            pltpu.VMEM((feats, TOK), jnp.bfloat16),
            pltpu.SemaphoreType.DMA((9,)),
        ],
        compiler_params=params(58),
        cost_estimate=cost(200_000_000, 3_000_000),
        name="prepare",
    )(frame_counts, query_rows, key_rows, value_rows, jnp.asarray(space), jnp.asarray(time), jnp.asarray(mats))

    pair = flip(kv, "yh")
    below = shift(kv, "z", 1)
    above = shift(kv, "z", -1)
    q_left = shift(q, "x", 1)
    q_right = shift(q, "x", -1)
    q_across = shift(q, "x", 2)
    q, kv = pl.pallas_call(
        stage_kernel,
        out_shape=[jax.ShapeDtypeStruct(v.shape, v.dtype) for v in (q, kv)],
        in_specs=[HBM] * 2,
        out_specs=[VMEM] * 2,
        scratch_shapes=[pltpu.SemaphoreType.DMA((2,))],
        compiler_params=params(8),
        cost_estimate=cost(1_000_000, 2_400_000),
        name="stage",
    )(q, kv)
    tp = lax.axis_index("yl") * 2 + lax.axis_index("core")
    cols = out_weight.shape[1] // 4

    def mine(j):
        return lax.dynamic_slice_in_dim(out_weight, j * cols, cols, 1)

    w_core = flip(mine(tp ^ 1), "core")
    pair, below, above, q_left, q_right, q_across, q, kv, w_core = lax.optimization_barrier(
        (pair, below, above, q_left, q_right, q_across, q, kv, w_core)
    )
    slant = [(zi * 2, (zi + 1) % 8 * 2) for zi in range(8)]
    slant += [(zi * 2 + 1, (zi - 1) % 8 * 2 + 1) for zi in range(8)]
    v_far = lax.ppermute(pair[feats:], ("z", "yh"), slant)
    k_far = flip(jnp.where(lax.axis_index("yh") == 1, below[:feats], above[:feats]), "yh")
    qs = [q, q_left, q_right, q_across]

    near_shape = jax.ShapeDtypeStruct((4, feats + 8 * HEADS, TOK), jnp.float32)
    near = pl.pallas_call(
        lambda *refs: attend_kernel(STEPS, False, *refs),
        out_shape=near_shape,
        in_specs=[SMEM] + [VMEM] * 7,
        out_specs=VMEM,
        scratch_shapes=[pltpu.VMEM((3, 2 * feats, TOK), jnp.bfloat16)],
        compiler_params=params(24),
        cost_estimate=cost(7_000_000_000, 5_000_000, 3_000_000),
        name="attend_near",
    )(frame_counts, *qs, below, kv, above)

    out = jax.ShapeDtypeStruct((feats + 16, TOK), jnp.bfloat16)
    partial = {}
    for block in CALLS:
        count = len(block)
        steps = [STEPS[r] for r in block]
        done = pl.pallas_call(
            lambda *refs, steps=steps: attend_kernel(steps, True, *refs),
            out_shape=[out] * count,
            in_specs=[SMEM] + [VMEM] * (count + 4),
            out_specs=[VMEM] * count,
            scratch_shapes=[pltpu.VMEM((2, 2 * feats, TOK), jnp.bfloat16)],
            compiler_params=params(24),
            cost_estimate=cost((1 + 2 * count) * 1_100_000_000, 3_000_000, count * 800_000),
            name="attend_far",
        )(frame_counts, *[qs[r] for r in block], pair, k_far, v_far, near)
        partial.update(zip(block, done))
        if block != CALLS[-1]:
            near, partial[block[0]] = lax.optimization_barrier((near, partial[block[0]]))

    out_weight, partial[1] = lax.optimization_barrier((out_weight, partial[1]))
    w_own = mine(tp)
    w_yl = flip(mine(tp ^ 2), "yl")
    w_far = lax.ppermute(mine(tp ^ 3), ("yh", "yl", "core"), [(i, 7 - i) for i in range(8)])
    across = shift(partial[3], "x", 2)
    left = shift(partial[1], "x", -1)
    right = shift(partial[2], "x", 1)
    merged = pl.pallas_call(
        merge_two_kernel,
        out_shape=jax.ShapeDtypeStruct((feats + 8 * HEADS, TOK), jnp.float32),
        in_specs=[VMEM] * 2,
        out_specs=VMEM,
        compiler_params=params(8),
        cost_estimate=cost(6_000_000_000, 2_000_000),
        name="merge_two",
    )(partial[0], across)
    att = pl.pallas_call(
        merge_last_kernel,
        out_shape=jax.ShapeDtypeStruct((TOK, feats), jnp.bfloat16),
        in_specs=[VMEM] * 3,
        out_specs=VMEM,
        compiler_params=params(8),
        cost_estimate=cost(30_000_000, 2_000_000),
        name="merge_last",
    )(merged, left, right)
    att_yl = flip(att, "yl")
    att_core = flip(att, "core")
    att_yl, w_yl, w_far = lax.optimization_barrier((att_yl, w_yl, w_far))
    att_far = flip(att_yl, "core")

    def add_terms(before, pairs, dtype):
        operands = ([] if before is None else [before]) + [v for pair in pairs for v in pair]
        tile = 256
        blocks = [pl.BlockSpec((tile, v.shape[1]), lambda i: (i, 0)) for v in operands[: len(operands) % 2]]
        for _ in pairs:
            blocks += [pl.BlockSpec((tile, feats), lambda i: (i, 0)), VMEM]
        return pl.pallas_call(
            project_kernel,
            grid=(TOK // tile,),
            out_shape=jax.ShapeDtypeStruct((TOK, cols), dtype),
            in_specs=blocks,
            out_specs=pl.BlockSpec((tile, cols), lambda i: (i, 0)),
            compiler_params=params(16),
            cost_estimate=cost(600_000_000 * len(pairs), 1_000_000),
            name="project",
        )(*operands)

    total = add_terms(None, [(att, w_own), (att_core, w_core)], jnp.float32)
    total = add_terms(total, [(att_yl, w_yl)], jnp.float32)
    return add_terms(total, [(att_far, w_far)], jnp.bfloat16)


def solution(mesh):
    fine = Mesh(mesh.devices.reshape(8, 2, 4, 2, 2), ("z", "yh", "x", "yl", "core"))
    seq, tp = ("z", "yh", "x"), ("yl", "core")
    return jax.shard_map(
        per_device,
        mesh=fine,
        in_specs=(P(seq, tp), P(seq, tp), P(seq, tp), P(), P(tp, None)),
        out_specs=P(seq, tp),
        check_vma=False,
    )
```

```python
import math

import jax
import jax.numpy as jnp
import numpy as np
from jax import lax
from jax.experimental import pallas as pl
from jax.experimental.pallas import tpu as pltpu
from jax.sharding import Mesh
from jax.sharding import PartitionSpec as P

RT = 16
RH = 56
RW = 56
PH = 16
PW = 16
FRAME = PH * PW
HEAD_DIM = 128
CLIPS = 12
HEADS = 3
TOK = 512
SLOTS = 16
ROPE_BASE = 256.0
NEG = -1e30
EXP_SCALE = HEAD_DIM ** (-0.5) * math.log2(math.e)

STEPS = (0, -1, 1, 2)
CALLS = ((3,), (1, 2), (0,))
COSTS = {0: 2, 1: 5, 3: 0.01}


def rope_tables():
    freq = np.zeros(HEAD_DIM)
    swap = np.zeros((HEAD_DIM, HEAD_DIM), np.float32)
    sign = np.zeros(HEAD_DIM)
    base = 0
    bounds = []
    for width in (RT, RH, RW):
        half = width // 2
        f = np.exp(-(2.0 * np.arange(half) / width) * math.log(ROPE_BASE))
        freq[base : base + half] = f
        freq[base + half : base + width] = f
        sign[base : base + half] = -1.0
        sign[base + half : base + width] = 1.0
        for j in range(half):
            swap[base + half + j, base + j] = 1.0
            swap[base + j, base + half + j] = 1.0
        bounds.append((base, base + width))
        base += width
    token = np.arange(FRAME)
    angle = np.zeros((FRAME, HEAD_DIM))
    (t0, t1), (h0, h1), (w0, w1) = bounds
    angle[:, h0:h1] = (token // PW)[:, None] * freq[None, h0:h1]
    angle[:, w0:w1] = (token % PW)[:, None] * freq[None, w0:w1]
    angle_t = np.zeros((SLOTS, HEAD_DIM))
    angle_t[:, t0:t1] = np.arange(SLOTS)[:, None] * freq[None, t0:t1]
    space = np.stack([np.cos(angle), np.sin(angle) * sign]).astype(np.float32)
    time = np.stack([np.cos(angle_t), np.sin(angle_t) * sign]).astype(np.float32)
    return space, time, swap


def here():
    return lax.axis_index("z"), lax.axis_index("yh"), lax.axis_index("x")


def clip_bounds(counts_ref, frame):
    start = jnp.int32(0)
    end = jnp.int32(0)
    total = jnp.int32(0)
    for c in range(CLIPS):
        past = frame >= total
        before = total
        total = total + counts_ref[c]
        start = jnp.where(past, before, start)
        end = jnp.where(past, total, end)
    return start, end


def dot_nt(a, b):
    return lax.dot_general(a, b, (((1,), (1,)), ((), ())), preferred_element_type=jnp.float32)


def dot_nn(a, b):
    return lax.dot_general(a, b, (((1,), (0,)), ((), ())), preferred_element_type=jnp.float32)


def prepare_kernel(counts_ref, q_hbm, k_hbm, v_hbm, space_hbm, time_hbm, swap_hbm, q_out, kv_out, *refs):
    bufs, (kv_buf, q_buf, sem) = refs[:-3], refs[-3:]
    sources = (k_hbm, space_hbm, time_hbm, swap_hbm, v_hbm, q_hbm)
    copies = [pltpu.make_async_copy(s, d, sem.at[i]) for i, (s, d) in enumerate(zip(sources, bufs))]
    for c in copies:
        c.start()
    k_ref, space_ref, time_ref, swap_ref, v_ref, q_ref = bufs
    z, yh, x = here()
    first = z * SLOTS + yh * 8 + x * 2
    times = []
    for e in range(2):
        start, _ = clip_bounds(counts_ref, first + e)
        times.append(jnp.clip(first + e - start, 0, SLOTS - 1))
    for c in copies[:4]:
        c.wait()
    swap = swap_ref[0]
    eye = swap_ref[1]
    lane = lax.broadcasted_iota(jnp.int32, (FRAME, HEAD_DIM), 1)
    tables = []
    for e in range(2):
        cos = jnp.where(lane < RT, time_ref[0, pl.ds(times[e], 1), :], space_ref[0])
        sin = jnp.where(lane < RT, time_ref[1, pl.ds(times[e], 1), :], space_ref[1])
        tables.append((cos, sin))
    parts = [
        (e, h, slice(FRAME * e, FRAME * (e + 1)), slice(HEAD_DIM * h, HEAD_DIM * (h + 1)))
        for h in range(HEADS)
        for e in range(2)
    ]
    for e, h, tok, col in parts:
        cos, sin = tables[e]
        k = k_ref[tok, col]
        rot = (k.astype(jnp.float32) * cos + dot_nn(k, swap) * sin).astype(jnp.bfloat16)
        kv_buf[col, FRAME * e : FRAME * e + 128] = rot[:128]
        kv_buf[col, FRAME * e + 128 : FRAME * e + 256] = rot[128:]
    outs = [pltpu.make_async_copy(kv_buf.at[pl.ds(0, HEADS * HEAD_DIM)], kv_out.at[pl.ds(0, HEADS * HEAD_DIM)], sem.at[6])]
    outs[0].start()
    copies[4].wait()
    for e, h, tok, col in parts:
        kv_buf[HEAD_DIM * (HEADS + h) : HEAD_DIM * (HEADS + h + 1), tok] = dot_nt(eye, v_ref[tok, col]).astype(jnp.bfloat16)
    values = pl.ds(HEADS * HEAD_DIM, HEADS * HEAD_DIM)
    outs.append(pltpu.make_async_copy(kv_buf.at[values], kv_out.at[values], sem.at[7]))
    outs[1].start()
    copies[5].wait()
    turned = [(cos.T, sin.T) for cos, sin in tables]
    for e, h, tok, col in parts:
        cos, sin = turned[e]
        q = q_ref[tok, col]
        q_buf[col, tok] = (dot_nt(eye, q) * cos + dot_nt(swap, q) * sin).astype(jnp.bfloat16)
    outs.append(pltpu.make_async_copy(q_buf, q_out, sem.at[8]))
    outs[2].start()
    for c in outs:
        c.wait()


def stage_kernel(q_hbm, kv_hbm, q_out, kv_out, sem):
    copies = [
        pltpu.make_async_copy(q_hbm, q_out, sem.at[0]),
        pltpu.make_async_copy(kv_hbm, kv_out, sem.at[1]),
    ]
    for c in copies:
        c.start()
    for c in copies:
        c.wait()


def split3(value):
    hi = value.astype(jnp.bfloat16)
    rest = value - hi.astype(jnp.float32)
    mid = rest.astype(jnp.bfloat16)
    low = (rest - mid.astype(jnp.float32)).astype(jnp.bfloat16)
    return [hi, mid, low]


def fold(value, op):
    out = value[0:8]
    for i in range(8, value.shape[0], 8):
        out = op(out, value[i : i + 8])
    return out


def attend_kernel(steps, final, counts_ref, *refs):
    n, count = HEADS, len(steps)
    q_refs, refs = refs[:count], refs[count:]
    kv_refs, refs = refs[:3], refs[3:]
    if final:
        near_ref, refs = refs[0], refs[1:]
        o_refs, (kv,) = refs[:count], refs[count:]
    else:
        near_ref, kv = refs

    def load(a):
        for part in range(2):
            row = slice(HEAD_DIM * (n * part + a), HEAD_DIM * (n * part + a + 1))
            if final:
                kv[0, row, :] = kv_refs[0][row, :]
                kv[1, row, :] = kv_refs[1 + part][HEAD_DIM * a : HEAD_DIM * (a + 1), :]
            else:
                for i in range(3):
                    kv[i, row, :] = kv_refs[i][row, :]

    z, yh, x = here()
    plane = z * SLOTS
    tables = []
    for r in range(count):
        xq = lax.rem(x + steps[r] + 4, 4)
        for e in range(2):
            start, end = clip_bounds(counts_ref, plane + yh * 8 + xq * 2 + e)
            places = []
            for sl in range(2):
                row = 1 - yh if final else yh
                mid = plane + row * 8 + x * 2 + sl
                before = mid - SLOTS >= start
                inside = (mid >= start) & (mid < end)
                after = mid + SLOTS < end
                if final:
                    src = jnp.where(inside, 0, 1)
                else:
                    src = jnp.where(inside, 1, jnp.where(before, 0, 2))
                valid = before | inside | after
                places.append((src, jnp.where(valid, 0.0, NEG), valid))
            tables.append((places, places[0][2] | places[1][2]))
    units = [(a, r, e) for a in range(n) for r in range(count) for e in range(2)]
    state, stats = {}, {}

    def scores(u, sl):
        a, r, e = units[u]
        if sl == 0 and r == 0 and e == 0:
            load(a)
        src, bias, _ = tables[2 * r + e][0][sl]
        row = slice(HEAD_DIM * a, HEAD_DIM * (a + 1))
        lo = FRAME * sl
        keys = jnp.concatenate([kv[src, row, lo : lo + 128], kv[src, row, lo + 128 : lo + 256]], axis=0)
        s = dot_nn(keys, q_refs[r][row, FRAME * e : FRAME * (e + 1)])
        peak = fold(s, jnp.maximum) * EXP_SCALE + bias
        st = state.setdefault(u, {"s": {}})
        st["s"][sl] = s
        st["top"] = peak if sl == 0 else jnp.maximum(st["top"], peak)

    def weigh(u, sl):
        a, r, e = units[u]
        places, some = tables[2 * r + e]
        src, bias, _ = places[sl]
        st = state[u]
        p = jnp.exp2(st["s"].pop(sl) * EXP_SCALE + jnp.where(some, bias - st["top"], NEG))
        add = fold(p, jnp.add)
        row = slice(HEAD_DIM * (n + a), HEAD_DIM * (n + a + 1))
        term = dot_nn(kv[src, row, FRAME * sl : FRAME * (sl + 1)], p.astype(jnp.bfloat16))
        st["total"] = add if sl == 0 else st["total"] + add
        st["acc"] = term if sl == 0 else st["acc"] + term

    def top(u):
        state[u]["top"] = jnp.max(state[u]["top"], axis=0, keepdims=True)

    for sl in range(2):
        scores(0, sl)
    top(0)
    for u, (a, r, e) in enumerate(units):
        for sl in range(2):
            if u + 1 < len(units):
                scores(u + 1, sl)
            weigh(u, sl)
        if u + 1 < len(units):
            top(u + 1)
        st = state.pop(u)
        total = jnp.sum(st["total"], axis=0, keepdims=True)
        peak = jnp.where(tables[2 * r + e][1], st["top"], NEG)
        row = slice(HEAD_DIM * a, HEAD_DIM * (a + 1))
        tok = slice(FRAME * e, FRAME * (e + 1))
        peak_row = slice(HEAD_DIM * n + 8 * a, HEAD_DIM * n + 8 * a + 1)
        total_row = slice(HEAD_DIM * n + 8 * a + 1, HEAD_DIM * n + 8 * a + 2)
        if final:
            block = STEPS.index(steps[r])
            near_peak = near_ref[block, peak_row, tok]
            both = jnp.maximum(peak, near_peak)
            far_part = jnp.exp2(peak - both)
            near_part = jnp.exp2(near_peak - both)
            total = total * far_part + near_ref[block, total_row, tok] * near_part
            total = jnp.maximum(total, 1e-30)
            inv = 1.0 / total
            acc = st["acc"] * (far_part * inv) + near_ref[block, row, tok] * (near_part * inv)
            o_refs[r][row, tok] = acc.astype(jnp.bfloat16)
            stats[r, a, e] = both + jnp.log2(total)
        else:
            near_ref[r, row, tok] = st["acc"]
            near_ref[r, peak_row, tok] = peak
            near_ref[r, total_row, tok] = total
    if final:
        for r in range(count):
            rows = []
            for a in range(n):
                rows += split3(jnp.concatenate([stats[r, a, 0], stats[r, a, 1]], axis=1))
            rows.append(jnp.zeros((16 - len(rows), TOK), jnp.bfloat16))
            o_refs[r][HEAD_DIM * n : HEAD_DIM * n + 16, :] = jnp.concatenate(rows, axis=0)


def level(ref, a):
    base = HEAD_DIM * HEADS
    tail = ref[base : base + 16, :].astype(jnp.float32)
    return tail[3 * a : 3 * a + 1] + tail[3 * a + 1 : 3 * a + 2] + tail[3 * a + 2 : 3 * a + 3]


def merge_two_kernel(p0, p1, out):
    for a in range(HEADS):
        row = slice(HEAD_DIM * a, HEAD_DIM * (a + 1))
        one, two = level(p0, a), level(p1, a)
        top = jnp.maximum(one, two)
        one, two = jnp.exp2(one - top), jnp.exp2(two - top)
        inv = 1.0 / (one + two)
        out[row, :] = p0[row, :].astype(jnp.float32) * (one * inv) + p1[row, :].astype(jnp.float32) * (two * inv)
        out[HEAD_DIM * HEADS + 8 * a : HEAD_DIM * HEADS + 8 * a + 1, :] = top + jnp.log2(one + two)


def merge_last_kernel(m, p0, p1, out):
    for a in range(HEADS):
        row = slice(HEAD_DIM * a, HEAD_DIM * (a + 1))
        base = HEAD_DIM * HEADS + 8 * a
        levels = [m[base : base + 1, :], level(p0, a), level(p1, a)]
        top = jnp.maximum(jnp.maximum(levels[0], levels[1]), levels[2])
        shares = [jnp.exp2(v - top) for v in levels]
        inv = 1.0 / (shares[0] + shares[1] + shares[2])
        acc = None
        for p, s in zip((m, p0, p1), shares):
            term = p[row, :].astype(jnp.float32) * (s * inv)
            acc = term if acc is None else acc + term
        out[:, row] = acc.T.astype(jnp.bfloat16)


def project_kernel(*refs):
    refs, out = refs[:-1], refs[-1]
    acc = None
    if len(refs) % 2:
        acc, refs = refs[0][...], refs[1:]
    for i in range(0, len(refs), 2):
        term = dot_nn(refs[i][...], refs[i + 1][...])
        acc = term if acc is None else acc + term
    out[...] = acc.astype(out.dtype)


VMEM = pl.BlockSpec(memory_space=pltpu.VMEM)
SMEM = pl.BlockSpec(memory_space=pltpu.SMEM)
HBM = pl.BlockSpec(memory_space=pltpu.HBM)


def params(mib):
    return pltpu.CompilerParams(vmem_limit_bytes=mib * 1024 * 1024)


def cost(flops, size, trans=0):
    return pl.CostEstimate(flops=flops, bytes_accessed=size, transcendentals=trans)


def shift(value, axis, by):
    count = lax.axis_size(axis)
    return lax.ppermute(value, axis, [(i, (i + by) % count) for i in range(count)])


def flip(value, axis):
    return lax.ppermute(value, axis, [(0, 1), (1, 0)])


def per_device(query_rows, key_rows, value_rows, frame_counts, out_weight):
    space, time, swap = rope_tables()
    mats = np.stack([swap, np.eye(HEAD_DIM)]).astype(jnp.bfloat16)
    feats = HEADS * HEAD_DIM
    q, kv = pl.pallas_call(
        prepare_kernel,
        out_shape=[jax.ShapeDtypeStruct((size, TOK), jnp.bfloat16) for size in (feats, 2 * feats)],
        in_specs=[SMEM] + [HBM] * 6,
        out_specs=[HBM] * 2,
        scratch_shapes=[
            pltpu.VMEM(key_rows.shape, jnp.bfloat16),
            pltpu.VMEM(space.shape, jnp.float32),
            pltpu.VMEM(time.shape, jnp.float32),
            pltpu.VMEM(mats.shape, jnp.bfloat16),
            pltpu.VMEM(key_rows.shape, jnp.bfloat16),
            pltpu.VMEM(key_rows.shape, jnp.bfloat16),
            pltpu.VMEM((2 * feats, TOK), jnp.bfloat16),
            pltpu.VMEM((feats, TOK), jnp.bfloat16),
            pltpu.SemaphoreType.DMA((9,)),
        ],
        compiler_params=params(58),
        cost_estimate=cost(200_000_000, 3_000_000),
        name="prepare",
    )(frame_counts, query_rows, key_rows, value_rows, jnp.asarray(space), jnp.asarray(time), jnp.asarray(mats))

    pair = flip(kv, "yh")
    below = shift(kv, "z", 1)
    above = shift(kv, "z", -1)
    q_left = shift(q, "x", 1)
    q_right = shift(q, "x", -1)
    q_across = shift(q, "x", 2)
    q, kv = pl.pallas_call(
        stage_kernel,
        out_shape=[jax.ShapeDtypeStruct(v.shape, v.dtype) for v in (q, kv)],
        in_specs=[HBM] * 2,
        out_specs=[VMEM] * 2,
        scratch_shapes=[pltpu.SemaphoreType.DMA((2,))],
        compiler_params=params(8),
        cost_estimate=cost(1_000_000, 2_400_000),
        name="stage",
    )(q, kv)
    tp = lax.axis_index("yl") * 2 + lax.axis_index("core")
    cols = out_weight.shape[1] // 4

    def mine(j):
        return lax.dynamic_slice_in_dim(out_weight, j * cols, cols, 1)

    w_core = flip(mine(tp ^ 1), "core")
    pair, below, above, q_left, q_right, q_across, q, kv, w_core = lax.optimization_barrier(
        (pair, below, above, q_left, q_right, q_across, q, kv, w_core)
    )
    slant = [(zi * 2, (zi + 1) % 8 * 2) for zi in range(8)]
    slant += [(zi * 2 + 1, (zi - 1) % 8 * 2 + 1) for zi in range(8)]
    v_far = lax.ppermute(pair[feats:], ("z", "yh"), slant)
    k_far = flip(jnp.where(lax.axis_index("yh") == 1, below[:feats], above[:feats]), "yh")
    qs = [q, q_left, q_right, q_across]

    near_shape = jax.ShapeDtypeStruct((4, feats + 8 * HEADS, TOK), jnp.float32)
    near = pl.pallas_call(
        lambda *refs: attend_kernel(STEPS, False, *refs),
        out_shape=near_shape,
        in_specs=[SMEM] + [VMEM] * 7,
        out_specs=VMEM,
        scratch_shapes=[pltpu.VMEM((3, 2 * feats, TOK), jnp.bfloat16)],
        compiler_params=params(24),
        cost_estimate=cost(7_000_000_000, 5_000_000, 3_000_000),
        name="attend_near",
    )(frame_counts, *qs, below, kv, above)

    out = jax.ShapeDtypeStruct((feats + 16, TOK), jnp.bfloat16)
    partial = {}
    for block in CALLS:
        count = len(block)
        steps = [STEPS[r] for r in block]
        done = pl.pallas_call(
            lambda *refs, steps=steps: attend_kernel(steps, True, *refs),
            out_shape=[out] * count,
            in_specs=[SMEM] + [VMEM] * (count + 4),
            out_specs=[VMEM] * count,
            scratch_shapes=[pltpu.VMEM((2, 2 * feats, TOK), jnp.bfloat16)],
            compiler_params=params(24),
            cost_estimate=cost(int(COSTS[len(partial)] * 1e9), 100_000),
            name="attend_far",
        )(frame_counts, *[qs[r] for r in block], pair, k_far, v_far, near)
        partial.update(zip(block, done))
        if block != CALLS[-1]:
            near, partial[block[0]] = lax.optimization_barrier((near, partial[block[0]]))

    out_weight, partial[0] = lax.optimization_barrier((out_weight, partial[0]))
    w_own = mine(tp)
    w_yl = flip(mine(tp ^ 2), "yl")
    w_far = lax.ppermute(mine(tp ^ 3), ("yh", "yl", "core"), [(i, 7 - i) for i in range(8)])
    across = shift(partial[3], "x", 2)
    left = shift(partial[1], "x", -1)
    right = shift(partial[2], "x", 1)
    merged = pl.pallas_call(
        merge_two_kernel,
        out_shape=jax.ShapeDtypeStruct((feats + 8 * HEADS, TOK), jnp.float32),
        in_specs=[VMEM] * 2,
        out_specs=VMEM,
        compiler_params=params(8),
        cost_estimate=cost(6_000_000_000, 2_000_000),
        name="merge_two",
    )(partial[0], across)
    att = pl.pallas_call(
        merge_last_kernel,
        out_shape=jax.ShapeDtypeStruct((TOK, feats), jnp.bfloat16),
        in_specs=[VMEM] * 3,
        out_specs=VMEM,
        compiler_params=params(8),
        cost_estimate=cost(30_000_000, 2_000_000),
        name="merge_last",
    )(merged, left, right)
    att_yl = flip(att, "yl")
    att_core = flip(att, "core")
    att_yl, w_yl, w_far = lax.optimization_barrier((att_yl, w_yl, w_far))
    att_far = flip(att_yl, "core")

    def add_terms(before, pairs, dtype):
        operands = ([] if before is None else [before]) + [v for pair in pairs for v in pair]
        tile = 256
        blocks = [pl.BlockSpec((tile, v.shape[1]), lambda i: (i, 0)) for v in operands[: len(operands) % 2]]
        for _ in pairs:
            blocks += [pl.BlockSpec((tile, feats), lambda i: (i, 0)), VMEM]
        return pl.pallas_call(
            project_kernel,
            grid=(TOK // tile,),
            out_shape=jax.ShapeDtypeStruct((TOK, cols), dtype),
            in_specs=blocks,
            out_specs=pl.BlockSpec((tile, cols), lambda i: (i, 0)),
            compiler_params=params(16),
            cost_estimate=cost(600_000_000 * len(pairs), 1_000_000),
            name="project",
        )(*operands)

    total = add_terms(None, [(att, w_own), (att_core, w_core)], jnp.float32)
    total = add_terms(total, [(att_yl, w_yl)], jnp.float32)
    return add_terms(total, [(att_far, w_far)], jnp.bfloat16)


def solution(mesh):
    fine = Mesh(mesh.devices.reshape(8, 2, 4, 2, 2), ("z", "yh", "x", "yl", "core"))
    seq, tp = ("z", "yh", "x"), ("yl", "core")
    return jax.shard_map(
        per_device,
        mesh=fine,
        in_specs=(P(seq, tp), P(seq, tp), P(seq, tp), P(), P(tp, None)),
        out_specs=P(seq, tp),
        check_vma=False,
    )
```

```python
import math

import jax
import jax.numpy as jnp
import numpy as np
from jax import lax
from jax.experimental import pallas as pl
from jax.experimental.pallas import tpu as pltpu
from jax.sharding import Mesh
from jax.sharding import PartitionSpec as P

RT = 16
RH = 56
RW = 56
PH = 16
PW = 16
FRAME = PH * PW
HEAD_DIM = 128
CLIPS = 12
HEADS = 3
TOK = 512
SLOTS = 16
ROPE_BASE = 256.0
NEG = -1e30
EXP_SCALE = HEAD_DIM ** (-0.5) * math.log2(math.e)

STEPS = (0, -1, 1, 2)
CALLS = ((3,), (1, 2), (0,))
COSTS = {0: 2, 1: 5, 3: 0.01}


def rope_tables():
    freq = np.zeros(HEAD_DIM)
    swap = np.zeros((HEAD_DIM, HEAD_DIM), np.float32)
    sign = np.zeros(HEAD_DIM)
    base = 0
    bounds = []
    for width in (RT, RH, RW):
        half = width // 2
        f = np.exp(-(2.0 * np.arange(half) / width) * math.log(ROPE_BASE))
        freq[base : base + half] = f
        freq[base + half : base + width] = f
        sign[base : base + half] = -1.0
        sign[base + half : base + width] = 1.0
        for j in range(half):
            swap[base + half + j, base + j] = 1.0
            swap[base + j, base + half + j] = 1.0
        bounds.append((base, base + width))
        base += width
    token = np.arange(FRAME)
    angle = np.zeros((FRAME, HEAD_DIM))
    (t0, t1), (h0, h1), (w0, w1) = bounds
    angle[:, h0:h1] = (token // PW)[:, None] * freq[None, h0:h1]
    angle[:, w0:w1] = (token % PW)[:, None] * freq[None, w0:w1]
    angle_t = np.zeros((SLOTS, HEAD_DIM))
    angle_t[:, t0:t1] = np.arange(SLOTS)[:, None] * freq[None, t0:t1]
    space = np.stack([np.cos(angle), np.sin(angle) * sign]).astype(np.float32)
    time = np.stack([np.cos(angle_t), np.sin(angle_t) * sign]).astype(np.float32)
    return space, time, swap


def here():
    return lax.axis_index("z"), lax.axis_index("yh"), lax.axis_index("x")


def clip_bounds(counts_ref, frame):
    start = jnp.int32(0)
    end = jnp.int32(0)
    total = jnp.int32(0)
    for c in range(CLIPS):
        past = frame >= total
        before = total
        total = total + counts_ref[c]
        start = jnp.where(past, before, start)
        end = jnp.where(past, total, end)
    return start, end


def dot_nt(a, b):
    return lax.dot_general(a, b, (((1,), (1,)), ((), ())), preferred_element_type=jnp.float32)


def dot_nn(a, b):
    return lax.dot_general(a, b, (((1,), (0,)), ((), ())), preferred_element_type=jnp.float32)


def prepare_kernel(counts_ref, q_hbm, k_hbm, v_hbm, space_hbm, time_hbm, swap_hbm, q_out, kv_out, *refs):
    bufs, (kv_buf, q_buf, sem) = refs[:-3], refs[-3:]
    sources = (k_hbm, space_hbm, time_hbm, swap_hbm, v_hbm, q_hbm)
    copies = [pltpu.make_async_copy(s, d, sem.at[i]) for i, (s, d) in enumerate(zip(sources, bufs))]
    for c in copies:
        c.start()
    k_ref, space_ref, time_ref, swap_ref, v_ref, q_ref = bufs
    z, yh, x = here()
    first = z * SLOTS + yh * 8 + x * 2
    times = []
    for e in range(2):
        start, _ = clip_bounds(counts_ref, first + e)
        times.append(jnp.clip(first + e - start, 0, SLOTS - 1))
    for c in copies[:4]:
        c.wait()
    swap = swap_ref[0]
    eye = swap_ref[1]
    lane = lax.broadcasted_iota(jnp.int32, (FRAME, HEAD_DIM), 1)
    tables = []
    for e in range(2):
        cos = jnp.where(lane < RT, time_ref[0, pl.ds(times[e], 1), :], space_ref[0])
        sin = jnp.where(lane < RT, time_ref[1, pl.ds(times[e], 1), :], space_ref[1])
        tables.append((cos, sin))
    parts = [
        (e, h, slice(FRAME * e, FRAME * (e + 1)), slice(HEAD_DIM * h, HEAD_DIM * (h + 1)))
        for h in range(HEADS)
        for e in range(2)
    ]
    for e, h, tok, col in parts:
        cos, sin = tables[e]
        k = k_ref[tok, col]
        rot = (k.astype(jnp.float32) * cos + dot_nn(k, swap) * sin).astype(jnp.bfloat16)
        kv_buf[col, FRAME * e : FRAME * e + 128] = rot[:128]
        kv_buf[col, FRAME * e + 128 : FRAME * e + 256] = rot[128:]
    outs = [pltpu.make_async_copy(kv_buf.at[pl.ds(0, HEADS * HEAD_DIM)], kv_out.at[pl.ds(0, HEADS * HEAD_DIM)], sem.at[6])]
    outs[0].start()
    copies[4].wait()
    for e, h, tok, col in parts:
        kv_buf[HEAD_DIM * (HEADS + h) : HEAD_DIM * (HEADS + h + 1), tok] = dot_nt(eye, v_ref[tok, col]).astype(jnp.bfloat16)
    values = pl.ds(HEADS * HEAD_DIM, HEADS * HEAD_DIM)
    outs.append(pltpu.make_async_copy(kv_buf.at[values], kv_out.at[values], sem.at[7]))
    outs[1].start()
    copies[5].wait()
    turned = [(cos.T, sin.T) for cos, sin in tables]
    for e, h, tok, col in parts:
        cos, sin = turned[e]
        q = q_ref[tok, col]
        q_buf[col, tok] = (dot_nt(eye, q) * cos + dot_nt(swap, q) * sin).astype(jnp.bfloat16)
    outs.append(pltpu.make_async_copy(q_buf, q_out, sem.at[8]))
    outs[2].start()
    for c in outs:
        c.wait()


def stage_kernel(q_hbm, kv_hbm, q_out, kv_out, sem):
    copies = [
        pltpu.make_async_copy(q_hbm, q_out, sem.at[0]),
        pltpu.make_async_copy(kv_hbm, kv_out, sem.at[1]),
    ]
    for c in copies:
        c.start()
    for c in copies:
        c.wait()


def split3(value):
    hi = value.astype(jnp.bfloat16)
    rest = value - hi.astype(jnp.float32)
    mid = rest.astype(jnp.bfloat16)
    low = (rest - mid.astype(jnp.float32)).astype(jnp.bfloat16)
    return [hi, mid, low]


def fold(value, op):
    out = value[0:8]
    for i in range(8, value.shape[0], 8):
        out = op(out, value[i : i + 8])
    return out


def attend_kernel(steps, final, counts_ref, *refs):
    n, count = HEADS, len(steps)
    q_refs, refs = refs[:count], refs[count:]
    kv_refs, refs = refs[:3], refs[3:]
    if final:
        near_ref, refs = refs[0], refs[1:]
        o_refs, (kv,) = refs[:count], refs[count:]
    else:
        near_ref, kv = refs

    def load(a):
        for part in range(2):
            row = slice(HEAD_DIM * (n * part + a), HEAD_DIM * (n * part + a + 1))
            if final:
                kv[0, row, :] = kv_refs[0][row, :]
                kv[1, row, :] = kv_refs[1 + part][HEAD_DIM * a : HEAD_DIM * (a + 1), :]
            else:
                for i in range(3):
                    kv[i, row, :] = kv_refs[i][row, :]

    z, yh, x = here()
    plane = z * SLOTS
    tables = []
    for r in range(count):
        xq = lax.rem(x + steps[r] + 4, 4)
        for e in range(2):
            start, end = clip_bounds(counts_ref, plane + yh * 8 + xq * 2 + e)
            places = []
            for sl in range(2):
                row = 1 - yh if final else yh
                mid = plane + row * 8 + x * 2 + sl
                before = mid - SLOTS >= start
                inside = (mid >= start) & (mid < end)
                after = mid + SLOTS < end
                if final:
                    src = jnp.where(inside, 0, 1)
                else:
                    src = jnp.where(inside, 1, jnp.where(before, 0, 2))
                valid = before | inside | after
                places.append((src, jnp.where(valid, 0.0, NEG), valid))
            tables.append((places, places[0][2] | places[1][2]))
    units = [(a, r, e) for a in range(n) for r in range(count) for e in range(2)]
    state, stats = {}, {}

    def scores(u, sl):
        a, r, e = units[u]
        if sl == 0 and r == 0 and e == 0:
            load(a)
        src, bias, _ = tables[2 * r + e][0][sl]
        row = slice(HEAD_DIM * a, HEAD_DIM * (a + 1))
        lo = FRAME * sl
        keys = jnp.concatenate([kv[src, row, lo : lo + 128], kv[src, row, lo + 128 : lo + 256]], axis=0)
        s = dot_nn(keys, q_refs[r][row, FRAME * e : FRAME * (e + 1)])
        peak = fold(s, jnp.maximum) * EXP_SCALE + bias
        st = state.setdefault(u, {"s": {}})
        st["s"][sl] = s
        st["top"] = peak if sl == 0 else jnp.maximum(st["top"], peak)

    def weigh(u, sl):
        a, r, e = units[u]
        places, some = tables[2 * r + e]
        src, bias, _ = places[sl]
        st = state[u]
        p = jnp.exp2(st["s"].pop(sl) * EXP_SCALE + jnp.where(some, bias - st["top"], NEG))
        add = fold(p, jnp.add)
        row = slice(HEAD_DIM * (n + a), HEAD_DIM * (n + a + 1))
        term = dot_nn(kv[src, row, FRAME * sl : FRAME * (sl + 1)], p.astype(jnp.bfloat16))
        st["total"] = add if sl == 0 else st["total"] + add
        st["acc"] = term if sl == 0 else st["acc"] + term

    def top(u):
        state[u]["top"] = jnp.max(state[u]["top"], axis=0, keepdims=True)

    for sl in range(2):
        scores(0, sl)
    top(0)
    for u, (a, r, e) in enumerate(units):
        for sl in range(2):
            if u + 1 < len(units):
                scores(u + 1, sl)
            weigh(u, sl)
        if u + 1 < len(units):
            top(u + 1)
        st = state.pop(u)
        total = jnp.sum(st["total"], axis=0, keepdims=True)
        peak = jnp.where(tables[2 * r + e][1], st["top"], NEG)
        row = slice(HEAD_DIM * a, HEAD_DIM * (a + 1))
        tok = slice(FRAME * e, FRAME * (e + 1))
        peak_row = slice(HEAD_DIM * n + 8 * a, HEAD_DIM * n + 8 * a + 1)
        total_row = slice(HEAD_DIM * n + 8 * a + 1, HEAD_DIM * n + 8 * a + 2)
        if final:
            block = STEPS.index(steps[r])
            near_peak = near_ref[block, peak_row, tok]
            both = jnp.maximum(peak, near_peak)
            far_part = jnp.exp2(peak - both)
            near_part = jnp.exp2(near_peak - both)
            total = total * far_part + near_ref[block, total_row, tok] * near_part
            total = jnp.maximum(total, 1e-30)
            inv = 1.0 / total
            acc = st["acc"] * (far_part * inv) + near_ref[block, row, tok] * (near_part * inv)
            o_refs[r][row, tok] = acc.astype(jnp.bfloat16)
            stats[r, a, e] = both + jnp.log2(total)
        else:
            near_ref[r, row, tok] = st["acc"]
            near_ref[r, peak_row, tok] = peak
            near_ref[r, total_row, tok] = total
    if final:
        for r in range(count):
            rows = []
            for a in range(n):
                rows += split3(jnp.concatenate([stats[r, a, 0], stats[r, a, 1]], axis=1))
            rows.append(jnp.zeros((16 - len(rows), TOK), jnp.bfloat16))
            o_refs[r][HEAD_DIM * n : HEAD_DIM * n + 16, :] = jnp.concatenate(rows, axis=0)


def level(ref, a):
    base = HEAD_DIM * HEADS
    tail = ref[base : base + 16, :].astype(jnp.float32)
    return tail[3 * a : 3 * a + 1] + tail[3 * a + 1 : 3 * a + 2] + tail[3 * a + 2 : 3 * a + 3]


def merge_two_kernel(p0, p1, out):
    for a in range(HEADS):
        row = slice(HEAD_DIM * a, HEAD_DIM * (a + 1))
        one, two = level(p0, a), level(p1, a)
        top = jnp.maximum(one, two)
        one, two = jnp.exp2(one - top), jnp.exp2(two - top)
        inv = 1.0 / (one + two)
        out[row, :] = p0[row, :].astype(jnp.float32) * (one * inv) + p1[row, :].astype(jnp.float32) * (two * inv)
        out[HEAD_DIM * HEADS + 8 * a : HEAD_DIM * HEADS + 8 * a + 1, :] = top + jnp.log2(one + two)


def merge_last_kernel(m, p0, p1, out):
    for a in range(HEADS):
        row = slice(HEAD_DIM * a, HEAD_DIM * (a + 1))
        base = HEAD_DIM * HEADS + 8 * a
        levels = [m[base : base + 1, :], level(p0, a), level(p1, a)]
        top = jnp.maximum(jnp.maximum(levels[0], levels[1]), levels[2])
        shares = [jnp.exp2(v - top) for v in levels]
        inv = 1.0 / (shares[0] + shares[1] + shares[2])
        acc = None
        for p, s in zip((m, p0, p1), shares):
            term = p[row, :].astype(jnp.float32) * (s * inv)
            acc = term if acc is None else acc + term
        out[:, row] = acc.T.astype(jnp.bfloat16)


def project_kernel(*refs):
    refs, out = refs[:-1], refs[-1]
    acc = None
    if len(refs) % 2:
        acc, refs = refs[0][...], refs[1:]
    for i in range(0, len(refs), 2):
        term = dot_nn(refs[i][...], refs[i + 1][...])
        acc = term if acc is None else acc + term
    out[...] = acc.astype(out.dtype)


VMEM = pl.BlockSpec(memory_space=pltpu.VMEM)
SMEM = pl.BlockSpec(memory_space=pltpu.SMEM)
HBM = pl.BlockSpec(memory_space=pltpu.HBM)


def params(mib):
    return pltpu.CompilerParams(vmem_limit_bytes=mib * 1024 * 1024)


def cost(flops, size, trans=0):
    return pl.CostEstimate(flops=flops, bytes_accessed=size, transcendentals=trans)


def shift(value, axis, by):
    count = lax.axis_size(axis)
    return lax.ppermute(value, axis, [(i, (i + by) % count) for i in range(count)])


def flip(value, axis):
    return lax.ppermute(value, axis, [(0, 1), (1, 0)])


def per_device(query_rows, key_rows, value_rows, frame_counts, out_weight):
    space, time, swap = rope_tables()
    mats = np.stack([swap, np.eye(HEAD_DIM)]).astype(jnp.bfloat16)
    feats = HEADS * HEAD_DIM
    q, kv = pl.pallas_call(
        prepare_kernel,
        out_shape=[jax.ShapeDtypeStruct((size, TOK), jnp.bfloat16) for size in (feats, 2 * feats)],
        in_specs=[SMEM] + [HBM] * 6,
        out_specs=[HBM] * 2,
        scratch_shapes=[
            pltpu.VMEM(key_rows.shape, jnp.bfloat16),
            pltpu.VMEM(space.shape, jnp.float32),
            pltpu.VMEM(time.shape, jnp.float32),
            pltpu.VMEM(mats.shape, jnp.bfloat16),
            pltpu.VMEM(key_rows.shape, jnp.bfloat16),
            pltpu.VMEM(key_rows.shape, jnp.bfloat16),
            pltpu.VMEM((2 * feats, TOK), jnp.bfloat16),
            pltpu.VMEM((feats, TOK), jnp.bfloat16),
            pltpu.SemaphoreType.DMA((9,)),
        ],
        compiler_params=params(58),
        cost_estimate=cost(200_000_000, 3_000_000),
        name="prepare",
    )(frame_counts, query_rows, key_rows, value_rows, jnp.asarray(space), jnp.asarray(time), jnp.asarray(mats))

    pair = flip(kv, "yh")
    below = shift(kv, "z", 1)
    above = shift(kv, "z", -1)
    q_left = shift(q, "x", 1)
    q_right = shift(q, "x", -1)
    q_across = shift(q, "x", 2)
    q, kv = pl.pallas_call(
        stage_kernel,
        out_shape=[jax.ShapeDtypeStruct(v.shape, v.dtype) for v in (q, kv)],
        in_specs=[HBM] * 2,
        out_specs=[VMEM] * 2,
        scratch_shapes=[pltpu.SemaphoreType.DMA((2,))],
        compiler_params=params(8),
        cost_estimate=cost(1_000_000, 2_400_000),
        name="stage",
    )(q, kv)
    tp = lax.axis_index("yl") * 2 + lax.axis_index("core")
    cols = out_weight.shape[1] // 4

    def mine(j):
        return lax.dynamic_slice_in_dim(out_weight, j * cols, cols, 1)

    pair, below, above, q_left, q_right, q_across, q, kv = lax.optimization_barrier(
        (pair, below, above, q_left, q_right, q_across, q, kv)
    )
    slant = [(zi * 2, (zi + 1) % 8 * 2) for zi in range(8)]
    slant += [(zi * 2 + 1, (zi - 1) % 8 * 2 + 1) for zi in range(8)]
    v_far = lax.ppermute(pair[feats:], ("z", "yh"), slant)
    k_far = flip(jnp.where(lax.axis_index("yh") == 1, below[:feats], above[:feats]), "yh")
    qs = [q, q_left, q_right, q_across]

    near_shape = jax.ShapeDtypeStruct((4, feats + 8 * HEADS, TOK), jnp.float32)
    near = pl.pallas_call(
        lambda *refs: attend_kernel(STEPS, False, *refs),
        out_shape=near_shape,
        in_specs=[SMEM] + [VMEM] * 7,
        out_specs=VMEM,
        scratch_shapes=[pltpu.VMEM((3, 2 * feats, TOK), jnp.bfloat16)],
        compiler_params=params(24),
        cost_estimate=cost(7_000_000_000, 5_000_000, 3_000_000),
        name="attend_near",
    )(frame_counts, *qs, below, kv, above)

    near, early_weight = lax.optimization_barrier((near, out_weight))
    w_core = flip(lax.dynamic_slice_in_dim(early_weight, (tp ^ 1) * cols, cols, 1), "core")
    out = jax.ShapeDtypeStruct((feats + 16, TOK), jnp.bfloat16)
    partial = {}
    for block in CALLS:
        count = len(block)
        steps = [STEPS[r] for r in block]
        done = pl.pallas_call(
            lambda *refs, steps=steps: attend_kernel(steps, True, *refs),
            out_shape=[out] * count,
            in_specs=[SMEM] + [VMEM] * (count + 4),
            out_specs=[VMEM] * count,
            scratch_shapes=[pltpu.VMEM((2, 2 * feats, TOK), jnp.bfloat16)],
            compiler_params=params(24),
            cost_estimate=cost(int(COSTS[len(partial)] * 1e9), 100_000),
            name="attend_far",
        )(frame_counts, *[qs[r] for r in block], pair, k_far, v_far, near)
        partial.update(zip(block, done))
        if block != CALLS[-1]:
            near, partial[block[0]] = lax.optimization_barrier((near, partial[block[0]]))

    out_weight, partial[0] = lax.optimization_barrier((out_weight, partial[0]))
    w_own = mine(tp)
    w_yl = flip(mine(tp ^ 2), "yl")
    w_far = lax.ppermute(mine(tp ^ 3), ("yh", "yl", "core"), [(i, 7 - i) for i in range(8)])
    across = shift(partial[3], "x", 2)
    left = shift(partial[1], "x", -1)
    right = shift(partial[2], "x", 1)
    merged = pl.pallas_call(
        merge_two_kernel,
        out_shape=jax.ShapeDtypeStruct((feats + 8 * HEADS, TOK), jnp.float32),
        in_specs=[VMEM] * 2,
        out_specs=VMEM,
        compiler_params=params(8),
        cost_estimate=cost(6_000_000_000, 2_000_000),
        name="merge_two",
    )(partial[0], across)
    merged, w_core = lax.optimization_barrier((merged, w_core))
    att = pl.pallas_call(
        merge_last_kernel,
        out_shape=jax.ShapeDtypeStruct((TOK, feats), jnp.bfloat16),
        in_specs=[VMEM] * 3,
        out_specs=VMEM,
        compiler_params=params(8),
        cost_estimate=cost(30_000_000, 2_000_000),
        name="merge_last",
    )(merged, left, right)
    att_yl = flip(att, "yl")
    att_core = flip(att, "core")
    att_yl, w_yl, w_far = lax.optimization_barrier((att_yl, w_yl, w_far))
    att_far = flip(att_yl, "core")

    def add_terms(before, pairs, dtype):
        operands = ([] if before is None else [before]) + [v for pair in pairs for v in pair]
        tile = 256
        blocks = [pl.BlockSpec((tile, v.shape[1]), lambda i: (i, 0)) for v in operands[: len(operands) % 2]]
        for _ in pairs:
            blocks += [pl.BlockSpec((tile, feats), lambda i: (i, 0)), VMEM]
        return pl.pallas_call(
            project_kernel,
            grid=(TOK // tile,),
            out_shape=jax.ShapeDtypeStruct((TOK, cols), dtype),
            in_specs=blocks,
            out_specs=pl.BlockSpec((tile, cols), lambda i: (i, 0)),
            compiler_params=params(16),
            cost_estimate=cost(600_000_000 * len(pairs), 1_000_000),
            name="project",
        )(*operands)

    total = add_terms(None, [(att, w_own), (att_core, w_core)], jnp.float32)
    total = add_terms(total, [(att_yl, w_yl)], jnp.float32)
    return add_terms(total, [(att_far, w_far)], jnp.bfloat16)


def solution(mesh):
    fine = Mesh(mesh.devices.reshape(8, 2, 4, 2, 2), ("z", "yh", "x", "yl", "core"))
    seq, tp = ("z", "yh", "x"), ("yl", "core")
    return jax.shard_map(
        per_device,
        mesh=fine,
        in_specs=(P(seq, tp), P(seq, tp), P(seq, tp), P(), P(tp, None)),
        out_specs=P(seq, tp),
        check_vma=False,
    )
```

```python
import math

import jax
import jax.numpy as jnp
import numpy as np
from jax import lax
from jax.experimental import pallas as pl
from jax.experimental.pallas import tpu as pltpu
from jax.sharding import Mesh
from jax.sharding import PartitionSpec as P

RT = 16
RH = 56
RW = 56
PH = 16
PW = 16
FRAME = PH * PW
HEAD_DIM = 128
CLIPS = 12
HEADS = 3
TOK = 512
SLOTS = 16
ROPE_BASE = 256.0
NEG = -1e30
EXP_SCALE = HEAD_DIM ** (-0.5) * math.log2(math.e)

STEPS = (0, -1, 1, 2)
CALLS = ((3,), (1, 2), (0,))
COSTS = {0: 2, 1: 5, 3: 0.01}


def rope_tables():
    freq = np.zeros(HEAD_DIM)
    swap = np.zeros((HEAD_DIM, HEAD_DIM), np.float32)
    sign = np.zeros(HEAD_DIM)
    base = 0
    bounds = []
    for width in (RT, RH, RW):
        half = width // 2
        f = np.exp(-(2.0 * np.arange(half) / width) * math.log(ROPE_BASE))
        freq[base : base + half] = f
        freq[base + half : base + width] = f
        sign[base : base + half] = -1.0
        sign[base + half : base + width] = 1.0
        for j in range(half):
            swap[base + half + j, base + j] = 1.0
            swap[base + j, base + half + j] = 1.0
        bounds.append((base, base + width))
        base += width
    token = np.arange(FRAME)
    angle = np.zeros((FRAME, HEAD_DIM))
    (t0, t1), (h0, h1), (w0, w1) = bounds
    angle[:, h0:h1] = (token // PW)[:, None] * freq[None, h0:h1]
    angle[:, w0:w1] = (token % PW)[:, None] * freq[None, w0:w1]
    angle_t = np.zeros((SLOTS, HEAD_DIM))
    angle_t[:, t0:t1] = np.arange(SLOTS)[:, None] * freq[None, t0:t1]
    space = np.stack([np.cos(angle), np.sin(angle) * sign]).astype(np.float32)
    time = np.stack([np.cos(angle_t), np.sin(angle_t) * sign]).astype(np.float32)
    return space, time, swap


def here():
    return lax.axis_index("z"), lax.axis_index("yh"), lax.axis_index("x")


def clip_bounds(counts_ref, frame):
    start = jnp.int32(0)
    end = jnp.int32(0)
    total = jnp.int32(0)
    for c in range(CLIPS):
        past = frame >= total
        before = total
        total = total + counts_ref[c]
        start = jnp.where(past, before, start)
        end = jnp.where(past, total, end)
    return start, end


def dot_nt(a, b):
    return lax.dot_general(a, b, (((1,), (1,)), ((), ())), preferred_element_type=jnp.float32)


def dot_nn(a, b):
    return lax.dot_general(a, b, (((1,), (0,)), ((), ())), preferred_element_type=jnp.float32)


def prepare_kernel(counts_ref, q_hbm, k_hbm, v_hbm, space_hbm, time_hbm, swap_hbm, q_out, kv_out, *refs):
    bufs, (kv_buf, q_buf, sem) = refs[:-3], refs[-3:]
    sources = (k_hbm, space_hbm, time_hbm, swap_hbm, v_hbm, q_hbm)
    copies = [pltpu.make_async_copy(s, d, sem.at[i]) for i, (s, d) in enumerate(zip(sources, bufs))]
    for c in copies:
        c.start()
    k_ref, space_ref, time_ref, swap_ref, v_ref, q_ref = bufs
    z, yh, x = here()
    first = z * SLOTS + yh * 8 + x * 2
    times = []
    for e in range(2):
        start, _ = clip_bounds(counts_ref, first + e)
        times.append(jnp.clip(first + e - start, 0, SLOTS - 1))
    for c in copies[:4]:
        c.wait()
    swap = swap_ref[0]
    eye = swap_ref[1]
    lane = lax.broadcasted_iota(jnp.int32, (FRAME, HEAD_DIM), 1)
    tables = []
    for e in range(2):
        cos = jnp.where(lane < RT, time_ref[0, pl.ds(times[e], 1), :], space_ref[0])
        sin = jnp.where(lane < RT, time_ref[1, pl.ds(times[e], 1), :], space_ref[1])
        tables.append((cos, sin))
    parts = [
        (e, h, slice(FRAME * e, FRAME * (e + 1)), slice(HEAD_DIM * h, HEAD_DIM * (h + 1)))
        for h in range(HEADS)
        for e in range(2)
    ]
    for e, h, tok, col in parts:
        cos, sin = tables[e]
        k = k_ref[tok, col]
        rot = (k.astype(jnp.float32) * cos + dot_nn(k, swap) * sin).astype(jnp.bfloat16)
        kv_buf[col, FRAME * e : FRAME * e + 128] = rot[:128]
        kv_buf[col, FRAME * e + 128 : FRAME * e + 256] = rot[128:]
    outs = [pltpu.make_async_copy(kv_buf.at[pl.ds(0, HEADS * HEAD_DIM)], kv_out.at[pl.ds(0, HEADS * HEAD_DIM)], sem.at[6])]
    outs[0].start()
    copies[4].wait()
    for e, h, tok, col in parts:
        kv_buf[HEAD_DIM * (HEADS + h) : HEAD_DIM * (HEADS + h + 1), tok] = dot_nt(eye, v_ref[tok, col]).astype(jnp.bfloat16)
    values = pl.ds(HEADS * HEAD_DIM, HEADS * HEAD_DIM)
    outs.append(pltpu.make_async_copy(kv_buf.at[values], kv_out.at[values], sem.at[7]))
    outs[1].start()
    copies[5].wait()
    turned = [(cos.T, sin.T) for cos, sin in tables]
    for e, h, tok, col in parts:
        cos, sin = turned[e]
        q = q_ref[tok, col]
        q_buf[col, tok] = (dot_nt(eye, q) * cos + dot_nt(swap, q) * sin).astype(jnp.bfloat16)
    outs.append(pltpu.make_async_copy(q_buf, q_out, sem.at[8]))
    outs[2].start()
    for c in outs:
        c.wait()


def stage_kernel(q_hbm, kv_hbm, q_out, kv_out, sem):
    copies = [
        pltpu.make_async_copy(q_hbm, q_out, sem.at[0]),
        pltpu.make_async_copy(kv_hbm, kv_out, sem.at[1]),
    ]
    for c in copies:
        c.start()
    for c in copies:
        c.wait()


def split3(value):
    hi = value.astype(jnp.bfloat16)
    rest = value - hi.astype(jnp.float32)
    mid = rest.astype(jnp.bfloat16)
    low = (rest - mid.astype(jnp.float32)).astype(jnp.bfloat16)
    return [hi, mid, low]


def fold(value, op):
    out = value[0:8]
    for i in range(8, value.shape[0], 8):
        out = op(out, value[i : i + 8])
    return out


def attend_kernel(steps, final, counts_ref, *refs):
    n, count = HEADS, len(steps)
    q_refs, refs = refs[:count], refs[count:]
    kv_refs, refs = refs[:3], refs[3:]
    if final:
        near_ref, refs = refs[0], refs[1:]
        o_refs, (kv,) = refs[:count], refs[count:]
    else:
        near_ref, kv = refs

    def load(a):
        for part in range(2):
            row = slice(HEAD_DIM * (n * part + a), HEAD_DIM * (n * part + a + 1))
            if final:
                kv[0, row, :] = kv_refs[0][row, :]
                kv[1, row, :] = kv_refs[1 + part][HEAD_DIM * a : HEAD_DIM * (a + 1), :]
            else:
                for i in range(3):
                    kv[i, row, :] = kv_refs[i][row, :]

    z, yh, x = here()
    plane = z * SLOTS
    tables = []
    for r in range(count):
        xq = lax.rem(x + steps[r] + 4, 4)
        for e in range(2):
            start, end = clip_bounds(counts_ref, plane + yh * 8 + xq * 2 + e)
            places = []
            for sl in range(2):
                row = 1 - yh if final else yh
                mid = plane + row * 8 + x * 2 + sl
                before = mid - SLOTS >= start
                inside = (mid >= start) & (mid < end)
                after = mid + SLOTS < end
                if final:
                    src = jnp.where(inside, 0, 1)
                else:
                    src = jnp.where(inside, 1, jnp.where(before, 0, 2))
                valid = before | inside | after
                places.append((src, jnp.where(valid, 0.0, NEG), valid))
            tables.append((places, places[0][2] | places[1][2]))
    units = [(a, r, e) for a in range(n) for r in range(count) for e in range(2)]
    state, stats = {}, {}

    def scores(u, sl):
        a, r, e = units[u]
        if sl == 0 and r == 0 and e == 0:
            load(a)
        src, bias, _ = tables[2 * r + e][0][sl]
        row = slice(HEAD_DIM * a, HEAD_DIM * (a + 1))
        lo = FRAME * sl
        keys = jnp.concatenate([kv[src, row, lo : lo + 128], kv[src, row, lo + 128 : lo + 256]], axis=0)
        s = dot_nn(keys, q_refs[r][row, FRAME * e : FRAME * (e + 1)])
        peak = fold(s, jnp.maximum) * EXP_SCALE + bias
        st = state.setdefault(u, {"s": {}})
        st["s"][sl] = s
        st["top"] = peak if sl == 0 else jnp.maximum(st["top"], peak)

    def weigh(u, sl):
        a, r, e = units[u]
        places, some = tables[2 * r + e]
        src, bias, _ = places[sl]
        st = state[u]
        p = jnp.exp2(st["s"].pop(sl) * EXP_SCALE + jnp.where(some, bias - st["top"], NEG))
        add = fold(p, jnp.add)
        row = slice(HEAD_DIM * (n + a), HEAD_DIM * (n + a + 1))
        term = dot_nn(kv[src, row, FRAME * sl : FRAME * (sl + 1)], p.astype(jnp.bfloat16))
        st["total"] = add if sl == 0 else st["total"] + add
        st["acc"] = term if sl == 0 else st["acc"] + term

    def top(u):
        state[u]["top"] = jnp.max(state[u]["top"], axis=0, keepdims=True)

    for sl in range(2):
        scores(0, sl)
    top(0)
    for u, (a, r, e) in enumerate(units):
        for sl in range(2):
            if u + 1 < len(units):
                scores(u + 1, sl)
            weigh(u, sl)
        if u + 1 < len(units):
            top(u + 1)
        st = state.pop(u)
        total = jnp.sum(st["total"], axis=0, keepdims=True)
        peak = jnp.where(tables[2 * r + e][1], st["top"], NEG)
        row = slice(HEAD_DIM * a, HEAD_DIM * (a + 1))
        tok = slice(FRAME * e, FRAME * (e + 1))
        peak_row = slice(HEAD_DIM * n + 8 * a, HEAD_DIM * n + 8 * a + 1)
        total_row = slice(HEAD_DIM * n + 8 * a + 1, HEAD_DIM * n + 8 * a + 2)
        if final:
            block = STEPS.index(steps[r])
            near_peak = near_ref[block, peak_row, tok]
            both = jnp.maximum(peak, near_peak)
            far_part = jnp.exp2(peak - both)
            near_part = jnp.exp2(near_peak - both)
            total = total * far_part + near_ref[block, total_row, tok] * near_part
            total = jnp.maximum(total, 1e-30)
            inv = 1.0 / total
            acc = st["acc"] * (far_part * inv) + near_ref[block, row, tok] * (near_part * inv)
            o_refs[r][row, tok] = acc.astype(jnp.bfloat16)
            stats[r, a, e] = both + jnp.log2(total)
        else:
            near_ref[r, row, tok] = st["acc"]
            near_ref[r, peak_row, tok] = peak
            near_ref[r, total_row, tok] = total
    if final:
        for r in range(count):
            rows = []
            for a in range(n):
                rows += split3(jnp.concatenate([stats[r, a, 0], stats[r, a, 1]], axis=1))
            rows.append(jnp.zeros((16 - len(rows), TOK), jnp.bfloat16))
            o_refs[r][HEAD_DIM * n : HEAD_DIM * n + 16, :] = jnp.concatenate(rows, axis=0)


def level(ref, a):
    base = HEAD_DIM * HEADS
    tail = ref[base : base + 16, :].astype(jnp.float32)
    return tail[3 * a : 3 * a + 1] + tail[3 * a + 1 : 3 * a + 2] + tail[3 * a + 2 : 3 * a + 3]


def merge_two_kernel(p0, p1, out):
    for a in range(HEADS):
        row = slice(HEAD_DIM * a, HEAD_DIM * (a + 1))
        one, two = level(p0, a), level(p1, a)
        top = jnp.maximum(one, two)
        one, two = jnp.exp2(one - top), jnp.exp2(two - top)
        inv = 1.0 / (one + two)
        out[row, :] = p0[row, :].astype(jnp.float32) * (one * inv) + p1[row, :].astype(jnp.float32) * (two * inv)
        out[HEAD_DIM * HEADS + 8 * a : HEAD_DIM * HEADS + 8 * a + 1, :] = top + jnp.log2(one + two)


def merge_last_kernel(m, p0, p1, out):
    for a in range(HEADS):
        row = slice(HEAD_DIM * a, HEAD_DIM * (a + 1))
        base = HEAD_DIM * HEADS + 8 * a
        levels = [m[base : base + 1, :], level(p0, a), level(p1, a)]
        top = jnp.maximum(jnp.maximum(levels[0], levels[1]), levels[2])
        shares = [jnp.exp2(v - top) for v in levels]
        inv = 1.0 / (shares[0] + shares[1] + shares[2])
        acc = None
        for p, s in zip((m, p0, p1), shares):
            term = p[row, :].astype(jnp.float32) * (s * inv)
            acc = term if acc is None else acc + term
        out[:, row] = acc.T.astype(jnp.bfloat16)


def project_kernel(*refs):
    refs, out = refs[:-1], refs[-1]
    acc = None
    if len(refs) % 2:
        acc, refs = refs[0][...], refs[1:]
    for i in range(0, len(refs), 2):
        term = dot_nn(refs[i][...], refs[i + 1][...])
        acc = term if acc is None else acc + term
    out[...] = acc.astype(out.dtype)


VMEM = pl.BlockSpec(memory_space=pltpu.VMEM)
SMEM = pl.BlockSpec(memory_space=pltpu.SMEM)
HBM = pl.BlockSpec(memory_space=pltpu.HBM)


def params(mib):
    return pltpu.CompilerParams(vmem_limit_bytes=mib * 1024 * 1024)


def cost(flops, size, trans=0):
    return pl.CostEstimate(flops=flops, bytes_accessed=size, transcendentals=trans)


def shift(value, axis, by):
    count = lax.axis_size(axis)
    return lax.ppermute(value, axis, [(i, (i + by) % count) for i in range(count)])


def flip(value, axis):
    return lax.ppermute(value, axis, [(0, 1), (1, 0)])


def per_device(query_rows, key_rows, value_rows, frame_counts, out_weight):
    space, time, swap = rope_tables()
    mats = np.stack([swap, np.eye(HEAD_DIM)]).astype(jnp.bfloat16)
    feats = HEADS * HEAD_DIM
    q, kv = pl.pallas_call(
        prepare_kernel,
        out_shape=[jax.ShapeDtypeStruct((size, TOK), jnp.bfloat16) for size in (feats, 2 * feats)],
        in_specs=[SMEM] + [HBM] * 6,
        out_specs=[HBM] * 2,
        scratch_shapes=[
            pltpu.VMEM(key_rows.shape, jnp.bfloat16),
            pltpu.VMEM(space.shape, jnp.float32),
            pltpu.VMEM(time.shape, jnp.float32),
            pltpu.VMEM(mats.shape, jnp.bfloat16),
            pltpu.VMEM(key_rows.shape, jnp.bfloat16),
            pltpu.VMEM(key_rows.shape, jnp.bfloat16),
            pltpu.VMEM((2 * feats, TOK), jnp.bfloat16),
            pltpu.VMEM((feats, TOK), jnp.bfloat16),
            pltpu.SemaphoreType.DMA((9,)),
        ],
        compiler_params=params(58),
        cost_estimate=cost(200_000_000, 3_000_000),
        name="prepare",
    )(frame_counts, query_rows, key_rows, value_rows, jnp.asarray(space), jnp.asarray(time), jnp.asarray(mats))

    pair = flip(kv, "yh")
    below = shift(kv, "z", 1)
    above = shift(kv, "z", -1)
    q_left = shift(q, "x", 1)
    q_right = shift(q, "x", -1)
    q_across = shift(q, "x", 2)
    q, kv = pl.pallas_call(
        stage_kernel,
        out_shape=[jax.ShapeDtypeStruct(v.shape, v.dtype) for v in (q, kv)],
        in_specs=[HBM] * 2,
        out_specs=[VMEM] * 2,
        scratch_shapes=[pltpu.SemaphoreType.DMA((2,))],
        compiler_params=params(8),
        cost_estimate=cost(1_000_000, 2_400_000),
        name="stage",
    )(q, kv)
    tp = lax.axis_index("yl") * 2 + lax.axis_index("core")
    cols = out_weight.shape[1] // 4

    def mine(j):
        return lax.dynamic_slice_in_dim(out_weight, j * cols, cols, 1)

    pair, below, above, q_left, q_right, q_across, q, kv = lax.optimization_barrier(
        (pair, below, above, q_left, q_right, q_across, q, kv)
    )
    slant = [(zi * 2, (zi + 1) % 8 * 2) for zi in range(8)]
    slant += [(zi * 2 + 1, (zi - 1) % 8 * 2 + 1) for zi in range(8)]
    v_far = lax.ppermute(pair[feats:], ("z", "yh"), slant)
    k_far = flip(jnp.where(lax.axis_index("yh") == 1, below[:feats], above[:feats]), "yh")
    qs = [q, q_left, q_right, q_across]

    near_shape = jax.ShapeDtypeStruct((4, feats + 8 * HEADS, TOK), jnp.float32)
    near = pl.pallas_call(
        lambda *refs: attend_kernel(STEPS, False, *refs),
        out_shape=near_shape,
        in_specs=[SMEM] + [VMEM] * 7,
        out_specs=VMEM,
        scratch_shapes=[pltpu.VMEM((3, 2 * feats, TOK), jnp.bfloat16)],
        compiler_params=params(24),
        cost_estimate=cost(7_000_000_000, 5_000_000, 3_000_000),
        name="attend_near",
    )(frame_counts, *qs, below, kv, above)

    near, early_weight = lax.optimization_barrier((near, out_weight))
    w_core = flip(lax.dynamic_slice_in_dim(early_weight, (tp ^ 1) * cols, cols, 1), "core")
    out = jax.ShapeDtypeStruct((feats + 16, TOK), jnp.bfloat16)
    partial = {}
    for block in CALLS:
        count = len(block)
        steps = [STEPS[r] for r in block]
        done = pl.pallas_call(
            lambda *refs, steps=steps: attend_kernel(steps, True, *refs),
            out_shape=[out] * count,
            in_specs=[SMEM] + [VMEM] * (count + 4),
            out_specs=[VMEM] * count,
            scratch_shapes=[pltpu.VMEM((2, 2 * feats, TOK), jnp.bfloat16)],
            compiler_params=params(24),
            cost_estimate=cost(int(COSTS[len(partial)] * 1e9), 100_000),
            name="attend_far",
        )(frame_counts, *[qs[r] for r in block], pair, k_far, v_far, near)
        partial.update(zip(block, done))
        if block != CALLS[-1]:
            near, partial[block[0]] = lax.optimization_barrier((near, partial[block[0]]))

    out_weight, partial[0] = lax.optimization_barrier((out_weight, partial[0]))
    w_own = mine(tp)
    w_yl = flip(mine(tp ^ 2), "yl")
    w_far = lax.ppermute(mine(tp ^ 3), ("yh", "yl", "core"), [(i, 7 - i) for i in range(8)])
    across = shift(partial[3], "x", 2)
    left = shift(partial[1], "x", -1)
    right = shift(partial[2], "x", 1)
    merged = pl.pallas_call(
        merge_two_kernel,
        out_shape=jax.ShapeDtypeStruct((feats + 8 * HEADS, TOK), jnp.float32),
        in_specs=[VMEM] * 2,
        out_specs=VMEM,
        compiler_params=params(8),
        cost_estimate=cost(6_000_000_000, 2_000_000),
        name="merge_two",
    )(partial[0], across)
    merged, w_core = lax.optimization_barrier((merged, w_core))
    att = pl.pallas_call(
        merge_last_kernel,
        out_shape=jax.ShapeDtypeStruct((TOK, feats), jnp.bfloat16),
        in_specs=[VMEM] * 3,
        out_specs=VMEM,
        compiler_params=params(8),
        cost_estimate=cost(30_000_000, 2_000_000),
        name="merge_last",
    )(merged, left, right)
    att_yl = flip(att, "yl")
    att_core = flip(att, "core")
    def add_terms(before, pairs, dtype):
        operands = ([] if before is None else [before]) + [v for pair in pairs for v in pair]
        tile = 256
        blocks = [pl.BlockSpec((tile, v.shape[1]), lambda i: (i, 0)) for v in operands[: len(operands) % 2]]
        for _ in pairs:
            blocks += [pl.BlockSpec((tile, feats), lambda i: (i, 0)), VMEM]
        return pl.pallas_call(
            project_kernel,
            grid=(TOK // tile,),
            out_shape=jax.ShapeDtypeStruct((TOK, cols), dtype),
            in_specs=blocks,
            out_specs=pl.BlockSpec((tile, cols), lambda i: (i, 0)),
            compiler_params=params(16),
            cost_estimate=cost(600_000_000 * len(pairs), 1_000_000),
            name="project",
        )(*operands)

    total = add_terms(None, [(att, w_own), (att_core, w_core)], jnp.float32)
    att_yl, w_yl, w_far, total = lax.optimization_barrier((att_yl, w_yl, w_far, total))
    att_far = flip(att_yl, "core")
    total = add_terms(total, [(att_yl, w_yl)], jnp.float32)
    return add_terms(total, [(att_far, w_far)], jnp.bfloat16)


def solution(mesh):
    fine = Mesh(mesh.devices.reshape(8, 2, 4, 2, 2), ("z", "yh", "x", "yl", "core"))
    seq, tp = ("z", "yh", "x"), ("yl", "core")
    return jax.shard_map(
        per_device,
        mesh=fine,
        in_specs=(P(seq, tp), P(seq, tp), P(seq, tp), P(), P(tp, None)),
        out_specs=P(seq, tp),
        check_vma=False,
    )
```
